256 devices in a mesh: ta: 16 (over z, core), wa: 16 (over y, x).
Axes of the slice: x: 4, y: 4, z: 8, core: 2. Of those that a mesh axis runs over, the one named last changes fastest.
Arguments:
- amplitudes: float32 [96, 512, 512], P('wa', 'ta'), may hold values from -6 to 6
- integrals: float32 [96, 512, 32, 512], P('wa', None, 'ta'), may hold values from -0.02734375 to 0.02734375
- blockmap: int32 [96, 32, 8, 8], P('wa', 'ta'), may hold values 0 or 1
- irrep_occ: int32 [96], replicated, may hold values from 0 to 1, as said below
- irrep_virt: int32 [512], replicated, may hold values from 0 to 1, as said below
Outputs:
- cycle_term: float32 [512, 32, 512], P('wa', 'ta')
The draws below stay inside these ranges and needn't reach their ends.
Inputs may be any that keep to these rules, and one draw needn't show every extreme that they name: `irrep_occ`: labels are constant over each aligned group of 8 occupied orbitals. `irrep_virt`: labels are constant over each aligned block of 64 virtual orbitals.
All inputs are finite; a program needn't handle non-finite values. No bound on the sum of `blockmap` on one device may be relied on, other than what follows from the above.
Results may differ from the reference program's by a relative error of at most 0.00007.
Values sent between devices are 32-bit elements; how exact they have to be, the bound alone decides.
A program may use at most 128 MiB of HBM per device.

```python
import jax
import jax.numpy as jnp
from jax import lax

OCC = 96
V = 512
BLK = 64
NB = 8
J = 32


def block_labels(key, groups, width):
    bits = jax.random.randint(key, (groups,), 0, 2, dtype=jnp.int32)
    order = jax.random.permutation(jax.random.fold_in(key, 1), groups)
    places = jnp.arange(groups, dtype=jnp.int32)
    bits = jnp.where(places == order[0], jnp.int32(0), bits)
    bits = jnp.where(places == order[1], jnp.int32(1), bits)
    return jnp.repeat(bits, width)


def draw_irrep_occ(key, part):
    key = jax.random.fold_in(key, 11)
    return block_labels(key, OCC // 8, 8)


def draw_irrep_virt(key, part):
    key = jax.random.fold_in(key, 23)
    return block_labels(key, V // BLK, BLK)


def place_ends(values, own_key, least, top_value):
    longest = values.shape.index(max(values.shape))
    spots = []
    for shift in (0, 1):
        where = [jax.random.randint(jax.random.fold_in(own_key, axis), (), 0, length) for axis, length in enumerate(values.shape)]
        where[longest] = (where[longest] + shift) % values.shape[longest]
        spots.append(tuple(where))
    return values.at[spots[0]].set(least).at[spots[1]].set(top_value)


def block_scale(rng, extent, pieces, low, largest):
    def one(position, blocks):
        steps = jax.random.uniform(jax.random.fold_in(jax.random.fold_in(rng, 6), position), (blocks,), jnp.float32, low / len(pieces), largest / len(pieces))
        return jnp.repeat(jnp.exp(steps), extent[position] // blocks).reshape((-1,) + (1,) * (len(extent) - position - 1))

    loudness = one(*pieces[0])
    for cut in pieces[1:]:
        loudness = loudness * one(*cut)
    return loudness


def gaussian(stream_key, shape, scale, most, cuts=(), held_as=jnp.bfloat16):
    drawn = scale * jax.random.normal(stream_key, shape, jnp.float32)
    if cuts:
        drawn = drawn * block_scale(stream_key, shape, cuts, -0.22, 0.18)
    return jnp.clip(drawn, -most, most).astype(held_as)


def setup_inputs(seed: int = 0) -> dict:
    seeds = jax.random.split(jax.random.key(seed), 6)
    return {
        "amplitudes": gaussian(seeds[0], (OCC, V, V), 1.0, 6.0, ((0, 16), (1, 16)), jnp.float32),
        "integrals": gaussian(seeds[1], (OCC, V, J, V), (OCC * V) ** -0.5, 0.02734375, ((0, 16), (2, 16)), jnp.float32),
        "blockmap": place_ends((jax.random.randint(seeds[2], (OCC, J, NB, NB), 0, 3) < 2).astype(jnp.int32), jax.random.fold_in(seeds[2], 1), 0, 1),
        "irrep_occ": draw_irrep_occ(jax.random.fold_in(seeds[5], 71), 0),
        "irrep_virt": draw_irrep_virt(jax.random.fold_in(seeds[5], 71), 0),
    }


def reference(amplitudes, integrals, blockmap, irrep_occ, irrep_virt):
    parity = (irrep_occ[:, None, None] + irrep_virt[None, :, None] + irrep_virt[None, None, :]) % 2
    screened = jnp.where(parity == 0, amplitudes, jnp.float32(0.0))
    combined = 2.0 * screened - jnp.transpose(screened, (0, 2, 1))

    def one_column(index):
        plane = integrals[:, :, index, :]
        blocks = blockmap[:, index, :, :].astype(jnp.float32)
        spread = jnp.repeat(jnp.repeat(blocks, BLK, axis=1), BLK, axis=2)
        return jnp.einsum("kac,kcb->ab", combined, plane * spread, precision=lax.Precision.HIGHEST)

    result = lax.map(one_column, jnp.arange(J, dtype=jnp.int32))
    return jnp.transpose(result, (1, 0, 2))
```

```python
import functools

import jax
import jax.numpy as jnp
from jax import lax
from jax.experimental import pallas as pl
from jax.experimental.pallas import tpu as pltpu
from jax.sharding import PartitionSpec as P

MESH = pl.DeviceIdType.MESH
LAG = 2
OCC_L = 6
UNITS = 2 * OCC_L
CHIPS = 8
F32 = jnp.float32
BF16 = jnp.bfloat16
TICKS = UNITS + 4 * LAG
DELAY = 1 + 4 * LAG


def split(v):
    hi = v.astype(BF16)
    lo = (v - hi.astype(F32)).astype(BF16)
    return hi, lo


def kernel(amp, w, bm, lv, lo_ref, out, X, Wf, Wh, Wl, bmx, Ch, Cl, acc, RA, RB, RD, S, QA, QB, QD,
           w_sem, x_sem, right_recv, left_recv, sib_recv, ring_send, rs_send, rs_recv):
    t = lax.axis_index("ta")
    wi = lax.axis_index("wa")
    z, h = t // 2, t % 2
    y, x = wi // 4, wi % 4

    def chip(delta):
        return lax.rem(z + delta + CHIPS, CHIPS)

    z_right = {"ta": chip(1) * 2 + h}
    z_left = {"ta": chip(-1) * 2 + h}
    sibling = {"ta": z * 2 + (1 - h)}

    def step(i, delta):
        return lax.rem(i + delta + 4, 4)

    x_next, x_prev = {"wa": y * 4 + step(x, 1)}, {"wa": y * 4 + step(x, -1)}
    y_next, y_prev = {"wa": step(y, 1) * 4 + x}, {"wa": step(y, -1) * 4 + x}

    def rows(zz, hh):
        return pl.ds(pl.multiple_of(zz * 64 + hh * 32, 32), 32)

    own = [
        pltpu.make_async_copy(amp.at[:, :, pl.ds(256 * g, 256)], X.at[:, g, rows(z, h), :], x_sem.at[g])
        for g in range(2)
    ]
    for c in own:
        c.start()

    def w_copy(k):
        return pltpu.make_async_copy(w.at[k], Wf.at[k], w_sem.at[k])

    for k in range(OCC_L):
        w_copy(k).start()

    barrier = pltpu.get_barrier_semaphore()
    neighbours = (z_right, z_left, sibling, x_next, x_prev, y_next, y_prev)
    for d in neighbours:
        pl.semaphore_signal(barrier, inc=1, device_id=d, device_id_type=MESH)

    lane = lax.broadcasted_iota(jnp.int32, (8, 512), 1) // 64
    row = lax.broadcasted_iota(jnp.int32, (8, 512), 0)
    spread = jnp.where(lane == row, 1.0, 0.0).astype(BF16)
    blocks = bm[...].astype(F32).reshape(96, 8).astype(BF16)
    bmx[...] = jnp.dot(blocks, spread, preferred_element_type=F32).reshape(12, 8, 512)
    acc[...] = jnp.zeros_like(acc)

    for c in own:
        c.wait()
    pl.semaphore_wait(barrier, len(neighbours))

    def unit_copy(u, zz, recv_sem, dest, direction):
        ref = X.at[u // 2, u % 2, rows(zz, h), :]
        return pltpu.make_async_remote_copy(
            src_ref=ref, dst_ref=ref, send_sem=ring_send.at[direction], recv_sem=recv_sem,
            device_id=dest, device_id_type=MESH)

    def to_right(u, zz, d):
        return unit_copy(u, zz, right_recv.at[u * 5 + d], z_right, 0)

    def to_left(u, zz, d):
        return unit_copy(u, zz, left_recv.at[u * 5 + d], z_left, 1)

    def to_sibling(u, zz):
        return unit_copy(u, zz, sib_recv.at[u // 2], sibling, 2)

    def w_prep(k):
        for r in range(8):
            bt, j = r // 2, r % 2
            for cb in range(8):
                slab = Wf[k, pl.ds(cb * 512 + r, 64, stride=8), :]
                m = bmx[k * 2 + j, pl.ds(cb, 1), pl.ds(bt * 128, 128)]
                hi, lo = split(slab * m)
                Wh[k, pl.ds(cb * 64, 64), pl.ds(r * 128, 128)] = hi
                Wl[k, pl.ds(cb * 64, 64), pl.ds(r * 128, 128)] = lo

    def compute(k, mh):
        lk = lo_ref[wi * OCC_L + k]
        blk = lax.broadcasted_iota(jnp.int32, (1, 256), 1) // 64
        for g in range(2):
            labels = jnp.zeros((1, 256), jnp.int32)
            for i in range(4):
                labels = jnp.where(blk == i, lv[(4 * g + i) * 64], labels)
            bt = X[k, mh, pl.ds(256 * g, 256), :].T
            for i in range(4):
                a = X[k, g, pl.ds(pl.multiple_of(256 * mh + 64 * i, 64), 64), :]
                lz = lv[(4 * mh + i) * 64]
                mask = ((labels + (lz + lk)) & 1) == 0
                c = jnp.where(mask, 2.0 * a - bt[64 * i:64 * i + 64, :], 0.0)
                hi, lo = split(c)
                Ch[pl.ds(64 * i, 64), pl.ds(256 * g, 256)] = hi
                Cl[pl.ds(64 * i, 64), pl.ds(256 * g, 256)] = lo
        for nb in range(4):
            n = pl.ds(256 * nb, 256)
            wh = Wh[k, :, n]
            p = jnp.dot(Ch[...], wh, preferred_element_type=F32)
            p = p + jnp.dot(Cl[...], wh, preferred_element_type=F32)
            p = p + jnp.dot(Ch[...], Wl[k, :, n], preferred_element_type=F32)
            acc[pl.ds(2 * mh, 2), :, :, n] += p.reshape(2, 4, 32, 256)

    def tick(s, _):
        @pl.when(s < UNITS)
        def _():
            to_right(s, z, 1).start()
            to_left(s, z, 1).start()
            to_sibling(s, z).start()

        for d in range(1, 5):
            u = s - LAG * d
            inside = (u >= 0) & (u < UNITS)
            even = u % 2 == 0

            @pl.when(inside if d < 4 else inside & even)
            def _():
                zz = chip(-d)
                to_right(u, zz, d).wait_recv()
                if d < 3:
                    to_right(u, zz, d + 1).start()
                elif d == 3:
                    @pl.when(even)
                    def _():
                        to_right(u, zz, d + 1).start()
                to_sibling(u, zz).start()

            @pl.when(inside if d < 4 else inside & jnp.logical_not(even))
            def _():
                zz = chip(d)
                to_left(u, zz, d).wait_recv()
                if d < 3:
                    to_left(u, zz, d + 1).start()
                elif d == 3:
                    @pl.when(jnp.logical_not(even))
                    def _():
                        to_left(u, zz, d + 1).start()
                to_sibling(u, zz).start()

        @pl.when((s >= 1) & (s < 1 + OCC_L))
        def _():
            k = s - 1
            w_copy(k).wait()
            w_prep(k)

        v = s - DELAY

        @pl.when((v >= 0) & (v < UNITS))
        def _():
            k, mh = v // 2, v % 2

            @pl.when(mh == 0)
            def _():
                ref = X.at[k, 0]
                pltpu.make_async_copy(ref, ref, sib_recv.at[k]).wait()

            compute(k, mh)

        return 0

    lax.fori_loop(0, UNITS + DELAY, tick, 0)

    def ring_sum(me, nxt, prv, view, bufs, base, result):
        a, b, d = bufs

        def copy(src, dst, i, dest):
            return pltpu.make_async_remote_copy(
                src_ref=src, dst_ref=dst, send_sem=rs_send.at[base + i], recv_sem=rs_recv.at[base + i],
                device_id=dest, device_id_type=MESH)

        first = [
            copy(view(step(me, 2), 0), a.at[0], 0, nxt),
            copy(view(step(me, 2), 1), a.at[1], 1, prv),
            copy(view(step(me, 1), 1), b.at[1], 2, nxt),
            copy(view(step(me, -1), 0), b.at[0], 3, prv),
        ]
        second = [
            copy(view(step(me, 1), 0), d.at[0], 4, nxt),
            copy(view(step(me, -1), 1), d.at[1], 5, prv),
        ]

        def start():
            for c in first:
                c.start()

        def middle():
            for i in range(2):
                first[i].wait_recv()
                ref = view(step(me, 1 if i == 0 else -1), i)
                ref[...] = ref[...] + a[i]
                second[i].start()

        def finish():
            first[2].wait_recv()
            first[3].wait_recv()
            for i in range(2):
                second[i].wait_recv()
                result(i, view(me, i)[...] + b[i] + d[i])

        def drain():
            for c in first + second:
                c.wait_send()

        return start, middle, finish, drain

    def cols(half, i):
        return pl.ds(512 * half + 256 * i, 256)

    def keep(half):
        def result(i, value):
            S[half, i] = value
        return result

    def emit(half):
        def result(i, value):
            for q in range(2):
                out[:, 4 * half + 2 * i + q, :] = value[:, 128 * q:128 * q + 128]
        return result

    def bufs(refs, half):
        return [r.at[half] for r in refs]

    one = [
        ring_sum(x, x_next, x_prev, lambda i, s: acc.at[:, i, :, cols(0, s)], bufs((RA, RB, RD), 0), 0, keep(0)),
        ring_sum(y, y_next, y_prev, lambda i, s: acc.at[i, :, :, cols(1, s)], bufs((RA, RB, RD), 1), 6, keep(1)),
    ]
    two = [
        ring_sum(y, y_next, y_prev, lambda i, s: S.at[0, s, i], bufs((QA, QB, QD), 0), 12, emit(0)),
        ring_sum(x, x_next, x_prev, lambda i, s: S.at[1, s, i], bufs((QA, QB, QD), 1), 18, emit(1)),
    ]
    for p in one:
        p[0]()
    for p in one:
        p[1]()
    for p, q in zip(one, two):
        p[2]()
        q[0]()
    for q in two:
        q[1]()
    for q in two:
        q[2]()
    for p in one + two:
        p[3]()
    for i, ref in enumerate((X.at[:, 0, pl.ds(0, 224), :], X.at[:, 0, pl.ds(0, 224), :], X.at[:, :, pl.ds(0, 256), :])):
        pltpu.make_async_copy(ref, ref, ring_send.at[i]).wait()


def local(amplitudes, integrals, blockmap, irrep_occ, irrep_virt):
    w = integrals.reshape(6, 512, 2, 4, 128).transpose(0, 1, 3, 2, 4).reshape(6, 4096, 128)
    hbm = pl.BlockSpec(memory_space=pl.ANY)
    vmem = pl.BlockSpec(memory_space=pltpu.VMEM)
    smem = pl.BlockSpec(memory_space=pltpu.SMEM)
    DMA = pltpu.SemaphoreType.DMA
    out = pl.pallas_call(
        kernel,
        out_shape=jax.ShapeDtypeStruct((32, 8, 128), F32),
        in_specs=[hbm, hbm, vmem, smem, smem],
        out_specs=vmem,
        scratch_shapes=[
            pltpu.VMEM((6, 2, 512, 256), F32),
            pltpu.VMEM((6, 4096, 128), F32),
            pltpu.VMEM((6, 512, 1024), BF16),
            pltpu.VMEM((6, 512, 1024), BF16),
            pltpu.VMEM((12, 8, 512), F32),
            pltpu.VMEM((256, 512), BF16),
            pltpu.VMEM((256, 512), BF16),
            pltpu.VMEM((4, 4, 32, 1024), F32),
            pltpu.VMEM((2, 2, 4, 32, 256), F32),
            pltpu.VMEM((2, 2, 4, 32, 256), F32),
            pltpu.VMEM((2, 2, 4, 32, 256), F32),
            pltpu.VMEM((2, 2, 4, 32, 256), F32),
            pltpu.VMEM((2, 2, 32, 256), F32),
            pltpu.VMEM((2, 2, 32, 256), F32),
            pltpu.VMEM((2, 2, 32, 256), F32),
            DMA((6,)),
            DMA((2,)),
            DMA((UNITS * 5,)),
            DMA((UNITS * 5,)),
            DMA((6,)),
            DMA((3,)),
            DMA((24,)),
            DMA((24,)),
        ],
        cost_estimate=pl.CostEstimate(flops=10 ** 10, bytes_accessed=14 * 10 ** 6, transcendentals=0),
        compiler_params=pltpu.CompilerParams(
            collective_id=0, has_side_effects=True, vmem_limit_bytes=60 * 1024 * 1024),
    )(amplitudes, w, blockmap, irrep_virt, irrep_occ)
    return out.reshape(32, 4, 2, 128).transpose(0, 2, 1, 3).reshape(32, 2, 512)


def solution(mesh):
    in_specs = (P("wa", "ta", None), P("wa", None, "ta", None), P("wa", "ta", None, None), P(), P())
    out_specs = P("wa", "ta", None)
    return jax.shard_map(local, mesh=mesh, in_specs=in_specs, out_specs=out_specs, check_vma=False)
```

```python
import functools

import jax
import jax.numpy as jnp
from jax import lax
from jax.experimental import pallas as pl
from jax.experimental.pallas import tpu as pltpu
from jax.sharding import PartitionSpec as P

MESH = pl.DeviceIdType.MESH
K = 6
CHIPS = 8
NB = 8
F32 = jnp.float32
BF16 = jnp.bfloat16
LAG = 2
UNITS = 2 * K
DELAY = 1 + 4 * LAG
ROW = 16
SEL = 8 * ROW


def split(v):
    hi = v.astype(BF16)
    lo = (v - hi.astype(F32)).astype(BF16)
    return hi, lo


def kernel(m, s, amp, w, bm, lv, lo_ref, out, A, X, Wf, Vh, Vl, Wh, Wl, bmx, Z, Ch, Cl, accS, acc, RA, RB, RD, S, QD,
           tab, w_sem, x_sem, right_recv, left_recv, sib_recv, ring_send, rs_send, rs_recv):
    t = lax.axis_index("ta")
    wi = lax.axis_index("wa")
    z, h = t // 2, t % 2
    y, x = wi // 4, wi % 4
    mp = m + m % 2
    width = 64 * mp

    def chip(delta):
        return lax.rem(z + delta + CHIPS, CHIPS)

    z_right = {"ta": chip(1) * 2 + h}
    z_left = {"ta": chip(-1) * 2 + h}
    sibling = {"ta": z * 2 + (1 - h)}

    def step(i, delta):
        return lax.rem(i + delta + 4, 4)

    x_next, x_prev = {"wa": y * 4 + step(x, 1)}, {"wa": y * 4 + step(x, -1)}
    y_next, y_prev = {"wa": step(y, 1) * 4 + x}, {"wa": step(y, -1) * 4 + x}
    x_far, y_far = {"wa": y * 4 + step(x, 2)}, {"wa": step(y, 2) * 4 + x}

    own = pltpu.make_async_copy(amp, A, x_sem)
    own.start()

    def w_copy(k):
        return pltpu.make_async_copy(w.at[k], Wf.at[k], w_sem.at[k])

    for k in range(K):
        w_copy(k).start()

    barrier = pltpu.get_barrier_semaphore()
    neighbours = (z_right, z_left, sibling, x_next, x_prev, x_far, y_next, y_prev, y_far)
    for d in neighbours:
        pl.semaphore_signal(barrier, inc=1, device_id=d, device_id_type=MESH)

    labels = [lv[64 * b] for b in range(NB)]
    ones = sum(labels)
    large = jnp.where(ones > NB // 2, 1, 0)
    member = [jnp.where(l == large, 0, 1) for l in labels]
    small_before = [sum(member[:b]) if b else jnp.int32(0) for b in range(NB)]
    rank = [jnp.where(member[b] == 1, small_before[b], b - small_before[b]) for b in range(NB)]
    small = sum(member)
    for g in range(2):
        for i in range(NB):
            for b in range(ROW):
                hit = (member[b] == g) & (rank[b] == i) if i <= b < NB else None
                tab[g * SEL + i * ROW + b] = jnp.int32(0) if hit is None else jnp.where(hit, 1, 0)

    def chosen(g, i, b, shape):
        return jnp.broadcast_to(tab[g * SEL + i * ROW + b], shape) == 1

    def chosen_either(g, lk, i, b, shape):
        one, two = tab[g * SEL + i * ROW + b], tab[(1 - g) * SEL + i * ROW + b]
        return jnp.broadcast_to(one + lk * (two - one), shape) == 1

    def size(g, lk):
        one, two = (NB - small, small) if g == 0 else (small, NB - small)
        return one + lk * (two - one)

    def span(g):
        return NB - (m, s)[g] + 1

    widest = NB - min(m, s) + 1

    def label_of(k):
        return lo_ref[wi * K + k]

    half = lax.broadcasted_iota(jnp.int32, (16, 128), 1) < 64
    own.wait()
    mine = jnp.where(lv[z * 64] == large, 0, 1)

    def pack(k):
        lk = label_of(k)
        group = mine + lk - 2 * mine * lk
        packed = []
        for b in range(NB):
            top, low = A[k, pl.ds(0, 16), pl.ds(b // 2 * 128, 128)], A[k, pl.ds(16, 16), pl.ds(b // 2 * 128, 128)]
            if b % 2:
                top = pltpu.roll(top, 64, 1)
            else:
                low = pltpu.roll(low, 64, 1)
            packed.append(jnp.where(half, top, low))
        for j in range(m):
            value = jnp.zeros((16, 128), F32)
            for b in range(j, min(j + widest, NB)):
                value = jnp.where(chosen_either(0, group, j, b, (16, 128)), packed[b], value)
            X[k, t, pl.ds(16 * j, 16), :] = value

    def unit_copy(u, zz, recv_sem, dest, direction):
        ref = X.at[u, zz * 2 + h]
        return pltpu.make_async_remote_copy(
            src_ref=ref, dst_ref=ref, send_sem=ring_send.at[direction], recv_sem=recv_sem,
            device_id=dest, device_id_type=MESH)

    def to_right(u, zz, d):
        return unit_copy(u, zz, right_recv.at[u * 5 + d], z_right, 0)

    def to_left(u, zz, d):
        return unit_copy(u, zz, left_recv.at[u * 5 + d], z_left, 1)

    def to_sibling(u, zz):
        return unit_copy(u, zz, sib_recv.at[u], sibling, 2)

    def send_own(u, _):
        pack(u)

        @pl.when(u == 0)
        def _():
            pl.semaphore_wait(barrier, len(neighbours))

        to_right(u, z, 1).start()
        to_left(u, z, 1).start()
        to_sibling(u, z).start()
        return 0

    def forward(d):
        def units(i, _):
            for u, reach_right, reach_left in ((2 * i, 4, 3), (2 * i + 1, 3, 4)):
                for side, sign, reach in ((to_right, -1, reach_right), (to_left, 1, reach_left)):
                    side(u, chip(sign * d), d).wait_recv()

                    def pass_on():
                        side(u, chip(sign * d), d + 1).start()

                    if reach == 4:
                        pass_on()
                    else:
                        pl.when(d < 3)(pass_on)
                    to_sibling(u, chip(sign * d)).start()
            return 0

        lax.fori_loop(0, K // 2, units, 0)

    def last_hop(i):
        for u, side in ((2 * i, to_right), (2 * i + 1, to_left)):
            side(u, chip(4), 4).wait_recv()
            to_sibling(u, chip(4)).start()

    def w_prep(k):
        w_copy(k).wait()

        def block(i, _):
            for r in range(8):
                bt, j = r // 2, r % 2
                slab = Wf[k, pl.ds(i * 512 + r, 64, stride=8), :]
                mask = bmx[k * 2 + j, i, :, pl.ds(bt * 128, 128)]
                hi, lo = split(slab * jnp.concatenate([mask] * 8, axis=0))
                Vh[k, i, :, pl.ds(r * 128, 128)] = hi
                Vl[k, i, :, pl.ds(r * 128, 128)] = lo
            return 0

        lax.fori_loop(0, NB, block, 0)
        lk = label_of(k)
        for g in range(2):
            def arrange(i, _):
                at = pl.ds(pl.multiple_of((k % 2) * width + i * 64, 64), 64)
                hit = [chosen_either(g, lk, i, i + o, (64, 256)) for o in range(widest)]
                for V, W in ((Vh, Wh), (Vl, Wl)):
                    for c in range(4):
                        value = jnp.zeros((64, 256), BF16)
                        for o in range(widest):
                            value = jnp.where(hit[o], V[k, jnp.minimum(i + o, NB - 1), :, pl.ds(256 * c, 256)], value)
                        W[k // 2, g, at, pl.ds(256 * c, 256)] = value
                return 0

            lax.fori_loop(0, mp, arrange, 0)

    groups = ((0, m, 0), (1, s, 64 * m))

    def build(k):
        ref = X.at[k, pl.ds(0, CHIPS)]
        pltpu.make_async_copy(ref, ref, sib_recv.at[k]).wait()

        for g, count, row0 in groups:
            def unpack(i, _):
                for core in range(2):
                    value = jnp.zeros((16 * m, 128), F32)
                    for o in range(span(g)):
                        b = jnp.minimum(i + o, NB - 1)
                        value = jnp.where(chosen(g, i, i + o, (16 * m, 128)), X[k, 2 * b + core], value)
                    at = row0 + 64 * i + 32 * core
                    for p in range(mp // 2):
                        one = value[32 * p:32 * p + 16]
                        two = value[32 * p + 16:32 * p + 32] if 2 * p + 1 < m else jnp.zeros((16, 128), F32)
                        cols = pl.ds(128 * p, 128)
                        Z[pl.ds(pl.multiple_of(at, 16), 16), cols] = jnp.where(half, one, pltpu.roll(two, 64, 1))
                        Z[pl.ds(pl.multiple_of(at + 16, 16), 16), cols] = jnp.where(half, pltpu.roll(one, 64, 1), two)
                return 0

            lax.fori_loop(0, count, unpack, 0)
        lk = label_of(k)
        into = pl.ds(pl.multiple_of(width * (k % 2), 128), width)
        for g, count, row0 in groups:
            wide = 64 * (count + count % 2)
            big = Z[pl.ds(0, 64 * m), pl.ds(0, wide)]
            few = jnp.concatenate([Z[pl.ds(64 * m, 64 * s), pl.ds(0, wide)]] + [jnp.zeros((64, wide), F32)] * (m - s), axis=0)
            pick = jnp.broadcast_to(lk, (64 * m, wide)) == g
            turned = jnp.where(pick, big, few)
            if mp > m:
                turned = jnp.concatenate([turned, jnp.zeros((64, wide), F32)], axis=0)
            turned = turned.T
            keep = lax.broadcasted_iota(jnp.int32, (64, width), 1) < size(g, lk) * 64
            for i in range(count):
                a = Z[pl.ds(row0 + 64 * i, 64), :]
                c = jnp.where(keep, 2.0 * a - turned[64 * i:64 * i + 64, :], 0.0)
                hi, lo = split(c)
                Ch[k // 2, pl.ds(row0 + 64 * i, 64), into] = hi
                Cl[k // 2, pl.ds(row0 + 64 * i, 64), into] = lo

    def multiply(c):
        n = pl.ds(pl.multiple_of(c * 256, 256), 256)

        def pair(q, _):
            for g, count, row0 in groups:
                rows = pl.ds(row0, 64 * count)
                wh = Wh[q, g, :, n]
                p = jnp.dot(Ch[q, rows, :], wh, preferred_element_type=F32)
                p = p + jnp.dot(Cl[q, rows, :], wh, preferred_element_type=F32)
                p = p + jnp.dot(Ch[q, rows, :], Wl[q, g, :, n], preferred_element_type=F32)
                accS[rows, :] = jnp.where(q == 0, p, accS[rows, :] + p)
            return 0

        lax.fori_loop(0, K // 2, pair, 0)

    def unsort(c):
        cols = pl.ds(pl.multiple_of(256 * c, 256), 256)

        def body(b, _):
            value = jnp.zeros((64, 256), F32)
            for g, count, row0 in groups:
                for o in range(span(g)):
                    i = b - o
                    at = jnp.minimum(jnp.maximum(i, 0), count - 1)
                    rows = pl.ds(pl.multiple_of(row0 + 64 * at, 64), 64)
                    flag = tab[g * SEL + at * ROW + b]
                    inside = (i >= 0) & (i < count)
                    hit = jnp.broadcast_to(jnp.where(inside, flag, 0), (64, 256)) == 1
                    value = jnp.where(hit, accS[rows, :], value)
            acc[b // 2, pl.ds(2 * (b % 2), 2), :, cols] = value.reshape(2, 32, 256)
            return 0

        lax.fori_loop(0, NB, body, 0)

    lax.fori_loop(0, K, send_own, 0)
    lane = lax.broadcasted_iota(jnp.int32, (8, 512), 1) // 64
    row = lax.broadcasted_iota(jnp.int32, (8, 512), 0)
    spread = jnp.where(lane == row, 1.0, 0.0).astype(BF16)
    blocks = jnp.broadcast_to(bm[...].astype(F32).reshape(96, 1, 8), (96, 8, 8)).reshape(768, 8).astype(BF16)
    bmx[...] = jnp.dot(blocks, spread, preferred_element_type=F32).reshape(12, 8, 8, 512)

    accS[...] = jnp.zeros_like(accS)

    def stage(st, _):
        lax.fori_loop(2 * st, 2 * st + 2, lambda k, _: w_prep(k) or 0, 0)
        forward(st + 1)
        return 0

    lax.fori_loop(0, 3, stage, 0)

    def copy(src, dst, i, dest):
        return pltpu.make_async_remote_copy(
            src_ref=src, dst_ref=dst, send_sem=rs_send.at[i], recv_sem=rs_recv.at[i],
            device_id=dest, device_id_type=MESH)

    along = ((x, x_next, x_prev, x_far), (y, y_next, y_prev, y_far))

    def view(part, c, i, side):
        cols = pl.ds(pl.multiple_of(256 * c + 128 * part, 128), 128)
        two = pl.ds(2 * side, 2)
        return acc.at[two, i, :, cols] if part == 0 else acc.at[i, two, :, cols]

    def first_axis(part, c):
        me, nxt, prv, _ = along[part]
        base = (4 * part + c) * 9
        a, b, d = (r.at[part, c] for r in (RA, RB, RD))
        far, up, down = step(me, 2), step(me, 1), step(me, -1)
        through = [copy(view(part, c, far, 0), a.at[0], base, nxt), copy(view(part, c, far, 1), a.at[1], base + 1, prv)]
        plain = [copy(view(part, c, down, 0), b.at[0], base + 2, prv), copy(view(part, c, up, 1), b.at[1], base + 3, nxt)]
        added = [copy(view(part, c, up, 0), d.at[0], base + 4, nxt), copy(view(part, c, down, 1), d.at[1], base + 5, prv)]
        return through, plain, added

    def second_axis(part, c):
        me, nxt, prv, far = along[1 - part]
        base = (4 * part + c) * 9 + 6
        return [copy(S.at[part, c, step(me, i + 1)], QD.at[part, c, i], base + i, dest)
                for i, dest in enumerate((nxt, far, prv))]

    def begin(c):
        stages = [first_axis(part, c) for part in range(2)]
        for order in range(2):
            for part in range(2):
                for send in stages[part][order]:
                    send.start()

    def middle(c):
        for part in range(2):
            me = along[part][0]
            through, _, added = first_axis(part, c)
            for i in range(2):
                through[i].wait_recv()
                view(part, c, step(me, 1 - 2 * i), i)[...] += RA[part, c, i]
                added[i].start()

    def finish(c):
        for part in range(2):
            me = along[part][0]
            _, plain, added = first_axis(part, c)
            for i in range(2):
                plain[i].wait_recv()
                added[i].wait_recv()
                S[part, c, pl.ds(2 * i, 2)] = view(part, c, me, i)[...] + RB[part, c, i] + RD[part, c, i]
            for send in second_axis(part, c):
                send.start()

    def close(c):
        for part in range(2):
            for send in second_axis(part, c):
                send.wait_recv()
            total = S[part, c, along[1 - part][0]] + QD[part, c, 0] + QD[part, c, 1] + QD[part, c, 2]
            out[:, 2 * c + part, :] = total

    def pair(q, _):
        last_hop(q)
        lax.fori_loop(2 * q, 2 * q + 2, lambda k, _: build(k) or 0, 0)
        return 0

    lax.fori_loop(0, K // 2, pair, 0)

    def chunk(c, _):
        @pl.when(c < 4)
        def _():
            multiply(c)
            unsort(c)
            begin(c)

        @pl.when((c >= 1) & (c < 5))
        def _():
            middle(c - 1)

        @pl.when(c >= 2)
        def _():
            finish(c - 2)

        return 0

    lax.fori_loop(0, 6, chunk, 0)
    for c in range(4):
        close(c)

    def drain(c, _):
        for part in range(2):
            for sends in first_axis(part, c) + (second_axis(part, c),):
                for send in sends:
                    send.wait_send()
        return 0

    lax.fori_loop(0, 4, drain, 0)
    for i, ref in enumerate((X.at[pl.ds(0, 3), pl.ds(0, 7)], X.at[pl.ds(0, 3), pl.ds(0, 7)], X.at[:, pl.ds(0, 8)])):
        pltpu.make_async_copy(ref, ref, ring_send.at[i]).wait()


def call(m, s, cid, amplitudes, w, blockmap, irrep_virt, irrep_occ):
    hbm = pl.BlockSpec(memory_space=pl.ANY)
    vmem = pl.BlockSpec(memory_space=pltpu.VMEM)
    smem = pl.BlockSpec(memory_space=pltpu.SMEM)
    DMA = pltpu.SemaphoreType.DMA
    mp = m + m % 2
    rows = 64 * (m + s)
    out = pl.pallas_call(
        functools.partial(kernel, m, s),
        out_shape=jax.ShapeDtypeStruct((32, 8, 128), F32),
        in_specs=[hbm, hbm, vmem, smem, smem],
        out_specs=vmem,
        scratch_shapes=[
            pltpu.VMEM((K, 32, 512), F32),
            pltpu.VMEM((K, 16, 16 * m, 128), F32),
            pltpu.VMEM((K, 4096, 128), F32),
            pltpu.VMEM((K, NB, 64, 1024), BF16),
            pltpu.VMEM((K, NB, 64, 1024), BF16),
            pltpu.VMEM((K // 2, 2, 128 * mp, 1024), BF16),
            pltpu.VMEM((K // 2, 2, 128 * mp, 1024), BF16),
            pltpu.VMEM((12, 8, 8, 512), F32),
            pltpu.VMEM((rows, 64 * mp), F32),
            pltpu.VMEM((K // 2, rows, 128 * mp), BF16),
            pltpu.VMEM((K // 2, rows, 128 * mp), BF16),
            pltpu.VMEM((rows, 256), F32),
            pltpu.VMEM((4, 4, 32, 1024), F32),
            pltpu.VMEM((2, 4, 2, 2, 32, 128), F32),
            pltpu.VMEM((2, 4, 2, 2, 32, 128), F32),
            pltpu.VMEM((2, 4, 2, 2, 32, 128), F32),
            pltpu.VMEM((2, 4, 4, 32, 128), F32),
            pltpu.VMEM((2, 4, 3, 32, 128), F32),
            pltpu.SMEM((2 * SEL,), jnp.int32),
            DMA((K,)),
            DMA,
            DMA((K * 5,)),
            DMA((K * 5,)),
            DMA((K,)),
            DMA((3,)),
            DMA((72,)),
            DMA((72,)),
        ],
        cost_estimate=pl.CostEstimate(flops=10 ** 10, bytes_accessed=14 * 10 ** 6, transcendentals=0),
        compiler_params=pltpu.CompilerParams(
            collective_id=cid, has_side_effects=True, vmem_limit_bytes=60 * 1024 * 1024),
    )(amplitudes, w, blockmap, irrep_virt, irrep_occ)
    return out.reshape(32, 4, 2, 128).transpose(0, 2, 1, 3).reshape(32, 2, 512)


def dense_kernel(amp, w, bm, lv, lo_ref, out, X, Wf, Wh, Wl, bmx, Ch, Cl, acc, RA, RB, RD, S, QA, QB, QD,
           w_sem, x_sem, right_recv, left_recv, sib_recv, ring_send, rs_send, rs_recv):
    t = lax.axis_index("ta")
    wi = lax.axis_index("wa")
    z, h = t // 2, t % 2
    y, x = wi // 4, wi % 4

    def chip(delta):
        return lax.rem(z + delta + CHIPS, CHIPS)

    z_right = {"ta": chip(1) * 2 + h}
    z_left = {"ta": chip(-1) * 2 + h}
    sibling = {"ta": z * 2 + (1 - h)}

    def step(i, delta):
        return lax.rem(i + delta + 4, 4)

    x_next, x_prev = {"wa": y * 4 + step(x, 1)}, {"wa": y * 4 + step(x, -1)}
    y_next, y_prev = {"wa": step(y, 1) * 4 + x}, {"wa": step(y, -1) * 4 + x}

    def rows(zz, hh):
        return pl.ds(pl.multiple_of(zz * 64 + hh * 32, 32), 32)

    own = [
        pltpu.make_async_copy(amp.at[:, :, pl.ds(256 * g, 256)], X.at[:, g, rows(z, h), :], x_sem.at[g])
        for g in range(2)
    ]
    for c in own:
        c.start()

    def w_copy(k):
        return pltpu.make_async_copy(w.at[k], Wf.at[k], w_sem.at[k])

    for k in range(K):
        w_copy(k).start()

    barrier = pltpu.get_barrier_semaphore()
    neighbours = (z_right, z_left, sibling, x_next, x_prev, y_next, y_prev)
    for d in neighbours:
        pl.semaphore_signal(barrier, inc=1, device_id=d, device_id_type=MESH)

    lane = lax.broadcasted_iota(jnp.int32, (8, 512), 1) // 64
    row = lax.broadcasted_iota(jnp.int32, (8, 512), 0)
    spread = jnp.where(lane == row, 1.0, 0.0).astype(BF16)
    blocks = bm[...].astype(F32).reshape(96, 8).astype(BF16)
    bmx[...] = jnp.dot(blocks, spread, preferred_element_type=F32).reshape(12, 8, 512)
    acc[...] = jnp.zeros_like(acc)

    for c in own:
        c.wait()
    pl.semaphore_wait(barrier, len(neighbours))

    def unit_copy(u, zz, recv_sem, dest, direction):
        ref = X.at[u // 2, u % 2, rows(zz, h), :]
        return pltpu.make_async_remote_copy(
            src_ref=ref, dst_ref=ref, send_sem=ring_send.at[direction], recv_sem=recv_sem,
            device_id=dest, device_id_type=MESH)

    def to_right(u, zz, d):
        return unit_copy(u, zz, right_recv.at[u * 5 + d], z_right, 0)

    def to_left(u, zz, d):
        return unit_copy(u, zz, left_recv.at[u * 5 + d], z_left, 1)

    def to_sibling(u, zz):
        return unit_copy(u, zz, sib_recv.at[u // 2], sibling, 2)

    def w_prep(k):
        for r in range(8):
            bt, j = r // 2, r % 2
            for cb in range(8):
                slab = Wf[k, pl.ds(cb * 512 + r, 64, stride=8), :]
                m = bmx[k * 2 + j, pl.ds(cb, 1), pl.ds(bt * 128, 128)]
                hi, lo = split(slab * m)
                Wh[k, pl.ds(cb * 64, 64), pl.ds(r * 128, 128)] = hi
                Wl[k, pl.ds(cb * 64, 64), pl.ds(r * 128, 128)] = lo

    def compute(k, mh):
        lk = lo_ref[wi * K + k]
        blk = lax.broadcasted_iota(jnp.int32, (1, 256), 1) // 64
        for g in range(2):
            labels = jnp.zeros((1, 256), jnp.int32)
            for i in range(4):
                labels = jnp.where(blk == i, lv[(4 * g + i) * 64], labels)
            bt = X[k, mh, pl.ds(256 * g, 256), :].T
            for i in range(4):
                a = X[k, g, pl.ds(pl.multiple_of(256 * mh + 64 * i, 64), 64), :]
                lz = lv[(4 * mh + i) * 64]
                mask = ((labels + (lz + lk)) & 1) == 0
                c = jnp.where(mask, 2.0 * a - bt[64 * i:64 * i + 64, :], 0.0)
                hi, lo = split(c)
                Ch[pl.ds(64 * i, 64), pl.ds(256 * g, 256)] = hi
                Cl[pl.ds(64 * i, 64), pl.ds(256 * g, 256)] = lo
        for nb in range(4):
            n = pl.ds(256 * nb, 256)
            wh = Wh[k, :, n]
            p = jnp.dot(Ch[...], wh, preferred_element_type=F32)
            p = p + jnp.dot(Cl[...], wh, preferred_element_type=F32)
            p = p + jnp.dot(Ch[...], Wl[k, :, n], preferred_element_type=F32)
            acc[pl.ds(2 * mh, 2), :, :, n] += p.reshape(2, 4, 32, 256)

    def tick(s, _):
        @pl.when(s < UNITS)
        def _():
            to_right(s, z, 1).start()
            to_left(s, z, 1).start()
            to_sibling(s, z).start()

        for d in range(1, 5):
            u = s - LAG * d
            inside = (u >= 0) & (u < UNITS)
            even = u % 2 == 0

            @pl.when(inside if d < 4 else inside & even)
            def _():
                zz = chip(-d)
                to_right(u, zz, d).wait_recv()
                if d < 3:
                    to_right(u, zz, d + 1).start()
                elif d == 3:
                    @pl.when(even)
                    def _():
                        to_right(u, zz, d + 1).start()
                to_sibling(u, zz).start()

            @pl.when(inside if d < 4 else inside & jnp.logical_not(even))
            def _():
                zz = chip(d)
                to_left(u, zz, d).wait_recv()
                if d < 3:
                    to_left(u, zz, d + 1).start()
                elif d == 3:
                    @pl.when(jnp.logical_not(even))
                    def _():
                        to_left(u, zz, d + 1).start()
                to_sibling(u, zz).start()

        @pl.when((s >= 1) & (s < 1 + K))
        def _():
            k = s - 1
            w_copy(k).wait()
            w_prep(k)

        v = s - DELAY

        @pl.when((v >= 0) & (v < UNITS))
        def _():
            k, mh = v // 2, v % 2

            @pl.when(mh == 0)
            def _():
                ref = X.at[k, 0]
                pltpu.make_async_copy(ref, ref, sib_recv.at[k]).wait()

            compute(k, mh)

        return 0

    lax.fori_loop(0, UNITS + DELAY, tick, 0)

    def ring_sum(me, nxt, prv, view, bufs, base, result):
        a, b, d = bufs

        def copy(src, dst, i, dest):
            return pltpu.make_async_remote_copy(
                src_ref=src, dst_ref=dst, send_sem=rs_send.at[base + i], recv_sem=rs_recv.at[base + i],
                device_id=dest, device_id_type=MESH)

        first = [
            copy(view(step(me, 2), 0), a.at[0], 0, nxt),
            copy(view(step(me, 2), 1), a.at[1], 1, prv),
            copy(view(step(me, 1), 1), b.at[1], 2, nxt),
            copy(view(step(me, -1), 0), b.at[0], 3, prv),
        ]
        second = [
            copy(view(step(me, 1), 0), d.at[0], 4, nxt),
            copy(view(step(me, -1), 1), d.at[1], 5, prv),
        ]

        def start():
            for c in first:
                c.start()

        def middle():
            for i in range(2):
                first[i].wait_recv()
                ref = view(step(me, 1 if i == 0 else -1), i)
                ref[...] = ref[...] + a[i]
                second[i].start()

        def finish():
            first[2].wait_recv()
            first[3].wait_recv()
            for i in range(2):
                second[i].wait_recv()
                result(i, view(me, i)[...] + b[i] + d[i])

        def drain():
            for c in first + second:
                c.wait_send()

        return start, middle, finish, drain

    def cols(half, i):
        return pl.ds(512 * half + 256 * i, 256)

    def keep(half):
        def result(i, value):
            S[half, i] = value
        return result

    def emit(half):
        def result(i, value):
            for q in range(2):
                out[:, 4 * half + 2 * i + q, :] = value[:, 128 * q:128 * q + 128]
        return result

    def bufs(refs, half):
        return [r.at[half] for r in refs]

    one = [
        ring_sum(x, x_next, x_prev, lambda i, s: acc.at[:, i, :, cols(0, s)], bufs((RA, RB, RD), 0), 0, keep(0)),
        ring_sum(y, y_next, y_prev, lambda i, s: acc.at[i, :, :, cols(1, s)], bufs((RA, RB, RD), 1), 6, keep(1)),
    ]
    two = [
        ring_sum(y, y_next, y_prev, lambda i, s: S.at[0, s, i], bufs((QA, QB, QD), 0), 12, emit(0)),
        ring_sum(x, x_next, x_prev, lambda i, s: S.at[1, s, i], bufs((QA, QB, QD), 1), 18, emit(1)),
    ]
    for p in one:
        p[0]()
    for p in one:
        p[1]()
    for p, q in zip(one, two):
        p[2]()
        q[0]()
    for q in two:
        q[1]()
    for q in two:
        q[2]()
    for p in one + two:
        p[3]()
    for i, ref in enumerate((X.at[:, 0, pl.ds(0, 224), :], X.at[:, 0, pl.ds(0, 224), :], X.at[:, :, pl.ds(0, 256), :])):
        pltpu.make_async_copy(ref, ref, ring_send.at[i]).wait()


def dense_call(cid, amplitudes, w, blockmap, irrep_virt, irrep_occ):
    hbm = pl.BlockSpec(memory_space=pl.ANY)
    vmem = pl.BlockSpec(memory_space=pltpu.VMEM)
    smem = pl.BlockSpec(memory_space=pltpu.SMEM)
    DMA = pltpu.SemaphoreType.DMA
    out = pl.pallas_call(
        dense_kernel,
        out_shape=jax.ShapeDtypeStruct((32, 8, 128), F32),
        in_specs=[hbm, hbm, vmem, smem, smem],
        out_specs=vmem,
        scratch_shapes=[
            pltpu.VMEM((6, 2, 512, 256), F32),
            pltpu.VMEM((6, 4096, 128), F32),
            pltpu.VMEM((6, 512, 1024), BF16),
            pltpu.VMEM((6, 512, 1024), BF16),
            pltpu.VMEM((12, 8, 512), F32),
            pltpu.VMEM((256, 512), BF16),
            pltpu.VMEM((256, 512), BF16),
            pltpu.VMEM((4, 4, 32, 1024), F32),
            pltpu.VMEM((2, 2, 4, 32, 256), F32),
            pltpu.VMEM((2, 2, 4, 32, 256), F32),
            pltpu.VMEM((2, 2, 4, 32, 256), F32),
            pltpu.VMEM((2, 2, 4, 32, 256), F32),
            pltpu.VMEM((2, 2, 32, 256), F32),
            pltpu.VMEM((2, 2, 32, 256), F32),
            pltpu.VMEM((2, 2, 32, 256), F32),
            DMA((6,)),
            DMA((2,)),
            DMA((UNITS * 5,)),
            DMA((UNITS * 5,)),
            DMA((6,)),
            DMA((3,)),
            DMA((24,)),
            DMA((24,)),
        ],
        cost_estimate=pl.CostEstimate(flops=10 ** 10, bytes_accessed=14 * 10 ** 6, transcendentals=0),
        compiler_params=pltpu.CompilerParams(
            collective_id=cid, has_side_effects=True, vmem_limit_bytes=60 * 1024 * 1024),
    )(amplitudes, w, blockmap, irrep_virt, irrep_occ)
    return out.reshape(32, 4, 2, 128).transpose(0, 2, 1, 3).reshape(32, 2, 512)


SIZES = ((4, 4), (5, 3), (6, 2))


def local(amplitudes, integrals, blockmap, irrep_occ, irrep_virt):
    w = integrals.reshape(6, 512, 2, 4, 128).transpose(0, 1, 3, 2, 4).reshape(6, 4096, 128)
    ones = jnp.right_shift(jnp.sum(irrep_virt), 6)
    which = jnp.minimum(jnp.maximum(ones, NB - ones) - 4, len(SIZES))
    branches = [functools.partial(call, m, s, i) for i, (m, s) in enumerate(SIZES)]
    branches.append(functools.partial(dense_call, len(SIZES)))
    return lax.switch(which, branches, amplitudes, w, blockmap, irrep_virt, irrep_occ)


def solution(mesh):
    in_specs = (P("wa", "ta", None), P("wa", None, "ta", None), P("wa", "ta", None, None), P(), P())
    out_specs = P("wa", "ta", None)
    return jax.shard_map(local, mesh=mesh, in_specs=in_specs, out_specs=out_specs, check_vma=False)
```

```python
import functools

import jax
import jax.numpy as jnp
from jax import lax
from jax.experimental import pallas as pl
from jax.experimental.pallas import tpu as pltpu
from jax.sharding import PartitionSpec as P

MESH = pl.DeviceIdType.MESH
K = 6
CHIPS = 8
NB = 8
F32 = jnp.float32
BF16 = jnp.bfloat16
LAG = 2
UNITS = 2 * K
DELAY = 1 + 4 * LAG
FAR_RIGHT = (0, 2, 5)
EARLY = (((0, 1), (1, 1)), ((2, 1), (3, 1)), ((4, 1), (0, 2), (5, 1), (1, 2)), ((2, 2), (3, 2)),
         ((0, 3), (4, 2), (5, 2), (1, 3)), ((2, 3), (0, 4), (3, 3), (4, 3), (5, 3), (1, 4)))
LATE = (((2, 4),), ((3, 4),), ((5, 4), (4, 4)), (), (), ())
ROW = 16
SEL = 8 * ROW


def split(v):
    hi = v.astype(BF16)
    lo = (v - hi.astype(F32)).astype(BF16)
    return hi, lo


def kernel(m, s, amp, w, bm, lv, lo_ref, out, A, X, Wf, Vh, Vl, Wh, Wl, bmx, Z, Ch, Cl, accS, acc, RA, RB, RD, S, QD,
           tab, w_sem, x_sem, right_recv, left_recv, sib_recv, ring_send, rs_send, rs_recv):
    t = lax.axis_index("ta")
    wi = lax.axis_index("wa")
    z, h = t // 2, t % 2
    y, x = wi // 4, wi % 4
    mp = m + m % 2
    width = 64 * mp

    def chip(delta):
        return lax.rem(z + delta + CHIPS, CHIPS)

    z_right = {"ta": chip(1) * 2 + h}
    z_left = {"ta": chip(-1) * 2 + h}
    sibling = {"ta": z * 2 + (1 - h)}

    def step(i, delta):
        return lax.rem(i + delta + 4, 4)

    x_next, x_prev = {"wa": y * 4 + step(x, 1)}, {"wa": y * 4 + step(x, -1)}
    y_next, y_prev = {"wa": step(y, 1) * 4 + x}, {"wa": step(y, -1) * 4 + x}
    x_far, y_far = {"wa": y * 4 + step(x, 2)}, {"wa": step(y, 2) * 4 + x}

    own = pltpu.make_async_copy(amp, A, x_sem)
    own.start()

    def w_copy(k):
        return pltpu.make_async_copy(w.at[k], Wf.at[k], w_sem.at[k])

    for k in range(K):
        w_copy(k).start()

    barrier = pltpu.get_barrier_semaphore()
    neighbours = (z_right, z_left, sibling, x_next, x_prev, x_far, y_next, y_prev, y_far)
    for d in neighbours:
        pl.semaphore_signal(barrier, inc=1, device_id=d, device_id_type=MESH)

    labels = [lv[64 * b] for b in range(NB)]
    ones = sum(labels)
    large = jnp.where(ones > NB // 2, 1, 0)
    member = [jnp.where(l == large, 0, 1) for l in labels]
    small_before = [sum(member[:b]) if b else jnp.int32(0) for b in range(NB)]
    rank = [jnp.where(member[b] == 1, small_before[b], b - small_before[b]) for b in range(NB)]
    small = sum(member)
    for g in range(2):
        for i in range(NB):
            for b in range(ROW):
                hit = (member[b] == g) & (rank[b] == i) if i <= b < NB else None
                tab[g * SEL + i * ROW + b] = jnp.int32(0) if hit is None else jnp.where(hit, 1, 0)

    def chosen(g, i, b, shape):
        return jnp.broadcast_to(tab[g * SEL + i * ROW + b], shape) == 1

    def chosen_either(g, lk, i, b, shape):
        one, two = tab[g * SEL + i * ROW + b], tab[(1 - g) * SEL + i * ROW + b]
        return jnp.broadcast_to(one + lk * (two - one), shape) == 1

    def size(g, lk):
        one, two = (NB - small, small) if g == 0 else (small, NB - small)
        return one + lk * (two - one)

    def span(g):
        return NB - (m, s)[g] + 1

    widest = NB - min(m, s) + 1

    def label_of(k):
        return lo_ref[wi * K + k]

    half = lax.broadcasted_iota(jnp.int32, (16, 128), 1) < 64
    own.wait()
    mine = jnp.where(lv[z * 64] == large, 0, 1)

    def pack(k):
        lk = label_of(k)
        group = mine + lk - 2 * mine * lk
        packed = []
        for b in range(NB):
            top, low = A[k, pl.ds(0, 16), pl.ds(b // 2 * 128, 128)], A[k, pl.ds(16, 16), pl.ds(b // 2 * 128, 128)]
            if b % 2:
                top = pltpu.roll(top, 64, 1)
            else:
                low = pltpu.roll(low, 64, 1)
            packed.append(jnp.where(half, top, low))
        for j in range(m):
            value = jnp.zeros((16, 128), F32)
            for b in range(j, min(j + widest, NB)):
                value = jnp.where(chosen_either(0, group, j, b, (16, 128)), packed[b], value)
            X[k, t, pl.ds(16 * j, 16), :] = value

    def unit_copy(u, zz, recv_sem, dest, direction):
        ref = X.at[u, zz * 2 + h]
        return pltpu.make_async_remote_copy(
            src_ref=ref, dst_ref=ref, send_sem=ring_send.at[direction], recv_sem=recv_sem,
            device_id=dest, device_id_type=MESH)

    def to_right(u, zz, d):
        return unit_copy(u, zz, right_recv.at[u * 5 + d], z_right, 0)

    def to_left(u, zz, d):
        return unit_copy(u, zz, left_recv.at[u * 5 + d], z_left, 1)

    def to_sibling(u, zz):
        return unit_copy(u, zz, sib_recv.at[u], sibling, 2)

    def send_own(u, _):
        pack(u)

        @pl.when(u == 0)
        def _():
            pl.semaphore_wait(barrier, len(neighbours))

        to_right(u, z, 1).start()
        to_left(u, z, 1).start()
        to_sibling(u, z).start()
        return 0

    def forward(u, d):
        for side, sign, reach in ((to_right, -1, 4 if u in FAR_RIGHT else 3), (to_left, 1, 3 if u in FAR_RIGHT else 4)):
            if d <= reach:
                side(u, chip(sign * d), d).wait_recv()
                if d < reach:
                    side(u, chip(sign * d), d + 1).start()
                to_sibling(u, chip(sign * d)).start()

    def after(i, moves):
        for j, some in enumerate(moves):
            if some:
                @pl.when(i == j)
                def _():
                    for u, d in some:
                        forward(u, d)

    def w_prep(k):
        w_copy(k).wait()

        def block(i, _):
            for r in range(8):
                bt, j = r // 2, r % 2
                slab = Wf[k, pl.ds(i * 512 + r, 64, stride=8), :]
                mask = bmx[k * 2 + j, i, :, pl.ds(bt * 128, 128)]
                hi, lo = split(slab * jnp.concatenate([mask] * 8, axis=0))
                Vh[k, i, :, pl.ds(r * 128, 128)] = hi
                Vl[k, i, :, pl.ds(r * 128, 128)] = lo
            return 0

        lax.fori_loop(0, NB, block, 0)
        lk = label_of(k)
        for g in range(2):
            def arrange(i, _):
                at = pl.ds(pl.multiple_of((k % 2) * width + i * 64, 64), 64)
                hit = [chosen_either(g, lk, i, i + o, (64, 256)) for o in range(widest)]
                for V, W in ((Vh, Wh), (Vl, Wl)):
                    for c in range(4):
                        value = jnp.zeros((64, 256), BF16)
                        for o in range(widest):
                            value = jnp.where(hit[o], V[k, jnp.minimum(i + o, NB - 1), :, pl.ds(256 * c, 256)], value)
                        W[k // 2, g, at, pl.ds(256 * c, 256)] = value
                return 0

            lax.fori_loop(0, mp, arrange, 0)

    groups = ((0, m, 0), (1, s, 64 * m))

    def build(k):
        ref = X.at[k, pl.ds(0, CHIPS)]
        pltpu.make_async_copy(ref, ref, sib_recv.at[k]).wait()

        for g, count, row0 in groups:
            def unpack(i, _):
                for core in range(2):
                    value = jnp.zeros((16 * m, 128), F32)
                    for o in range(span(g)):
                        b = jnp.minimum(i + o, NB - 1)
                        value = jnp.where(chosen(g, i, i + o, (16 * m, 128)), X[k, 2 * b + core], value)
                    at = row0 + 64 * i + 32 * core
                    for p in range(mp // 2):
                        one = value[32 * p:32 * p + 16]
                        two = value[32 * p + 16:32 * p + 32] if 2 * p + 1 < m else jnp.zeros((16, 128), F32)
                        cols = pl.ds(128 * p, 128)
                        Z[pl.ds(pl.multiple_of(at, 16), 16), cols] = jnp.where(half, one, pltpu.roll(two, 64, 1))
                        Z[pl.ds(pl.multiple_of(at + 16, 16), 16), cols] = jnp.where(half, pltpu.roll(one, 64, 1), two)
                return 0

            lax.fori_loop(0, count, unpack, 0)
        lk = label_of(k)
        into = pl.ds(pl.multiple_of(width * (k % 2), 128), width)
        for g, count, row0 in groups:
            wide = 64 * (count + count % 2)
            big = Z[pl.ds(0, 64 * m), pl.ds(0, wide)]
            few = jnp.concatenate([Z[pl.ds(64 * m, 64 * s), pl.ds(0, wide)]] + [jnp.zeros((64, wide), F32)] * (m - s), axis=0)
            pick = jnp.broadcast_to(lk, (64 * m, wide)) == g
            turned = jnp.where(pick, big, few)
            if mp > m:
                turned = jnp.concatenate([turned, jnp.zeros((64, wide), F32)], axis=0)
            turned = turned.T
            keep = lax.broadcasted_iota(jnp.int32, (64, width), 1) < size(g, lk) * 64
            for i in range(count):
                a = Z[pl.ds(row0 + 64 * i, 64), :]
                c = jnp.where(keep, 2.0 * a - turned[64 * i:64 * i + 64, :], 0.0)
                hi, lo = split(c)
                Ch[k // 2, pl.ds(row0 + 64 * i, 64), into] = hi
                Cl[k // 2, pl.ds(row0 + 64 * i, 64), into] = lo

    def multiply(c):
        n = pl.ds(pl.multiple_of(c * 256, 256), 256)

        def pair(q, _):
            for g, count, row0 in groups:
                rows = pl.ds(row0, 64 * count)
                wh = Wh[q, g, :, n]
                p = jnp.dot(Ch[q, rows, :], wh, preferred_element_type=F32)
                p = p + jnp.dot(Cl[q, rows, :], wh, preferred_element_type=F32)
                p = p + jnp.dot(Ch[q, rows, :], Wl[q, g, :, n], preferred_element_type=F32)
                accS[rows, :] = jnp.where(q == 0, p, accS[rows, :] + p)
            return 0

        lax.fori_loop(0, K // 2, pair, 0)

    def unsort(c):
        cols = pl.ds(pl.multiple_of(256 * c, 256), 256)

        for b in range(NB):
            value = None
            for g, count, row0 in groups:
                for i in range(max(0, b - span(g) + 1), min(b + 1, count)):
                    rows = accS[pl.ds(row0 + 64 * i, 64), :]
                    value = rows if value is None else jnp.where(chosen(g, i, b, (64, 256)), rows, value)
            acc[b // 2, pl.ds(2 * (b % 2), 2), :, cols] = value.reshape(2, 32, 256)

    lax.fori_loop(0, K, send_own, 0)
    lane = lax.broadcasted_iota(jnp.int32, (8, 512), 1) // 64
    row = lax.broadcasted_iota(jnp.int32, (8, 512), 0)
    spread = jnp.where(lane == row, 1.0, 0.0).astype(BF16)
    blocks = jnp.broadcast_to(bm[...].astype(F32).reshape(96, 1, 8), (96, 8, 8)).reshape(768, 8).astype(BF16)
    bmx[...] = jnp.dot(blocks, spread, preferred_element_type=F32).reshape(12, 8, 8, 512)

    accS[...] = jnp.zeros_like(accS)

    def prepare(k, _):
        w_prep(k)
        after(k, EARLY)
        return 0

    lax.fori_loop(0, K, prepare, 0)

    def copy(src, dst, i, dest):
        return pltpu.make_async_remote_copy(
            src_ref=src, dst_ref=dst, send_sem=rs_send.at[i], recv_sem=rs_recv.at[i],
            device_id=dest, device_id_type=MESH)

    along = ((x, x_next, x_prev, x_far), (y, y_next, y_prev, y_far))

    def view(part, c, i, side):
        cols = pl.ds(pl.multiple_of(256 * c + 128 * part, 128), 128)
        two = pl.ds(2 * side, 2)
        return acc.at[two, i, :, cols] if part == 0 else acc.at[i, two, :, cols]

    def first_axis(part, c):
        me, nxt, prv, _ = along[part]
        base = (4 * part + c) * 9
        a, b, d = (r.at[part, c] for r in (RA, RB, RD))
        far, up, down = step(me, 2), step(me, 1), step(me, -1)
        through = [copy(view(part, c, far, 0), a.at[0], base, nxt), copy(view(part, c, far, 1), a.at[1], base + 1, prv)]
        plain = [copy(view(part, c, down, 0), b.at[0], base + 2, prv), copy(view(part, c, up, 1), b.at[1], base + 3, nxt)]
        added = [copy(view(part, c, up, 0), d.at[0], base + 4, nxt), copy(view(part, c, down, 1), d.at[1], base + 5, prv)]
        return through, plain, added

    def second_axis(part, c):
        me, nxt, prv, far = along[1 - part]
        base = (4 * part + c) * 9 + 6
        return [copy(S.at[part, c, step(me, i + 1)], QD.at[part, c, i], base + i, dest)
                for i, dest in enumerate((nxt, far, prv))]

    def begin(c):
        stages = [first_axis(part, c) for part in range(2)]
        for order in range(2):
            for part in range(2):
                for send in stages[part][order]:
                    send.start()

    def middle(c):
        for part in range(2):
            me = along[part][0]
            through, _, added = first_axis(part, c)
            for i in range(2):
                through[i].wait_recv()
                view(part, c, step(me, 1 - 2 * i), i)[...] += RA[part, c, i]
                added[i].start()

    def finish(c):
        for part in range(2):
            me = along[part][0]
            _, plain, added = first_axis(part, c)
            for i in range(2):
                plain[i].wait_recv()
                added[i].wait_recv()
                S[part, c, pl.ds(2 * i, 2)] = view(part, c, me, i)[...] + RB[part, c, i] + RD[part, c, i]
            for send in second_axis(part, c):
                send.start()

    def close(c):
        for part in range(2):
            for send in second_axis(part, c):
                send.wait_recv()
            total = S[part, c, along[1 - part][0]] + QD[part, c, 0] + QD[part, c, 1] + QD[part, c, 2]
            out[:, 2 * c + part, :] = total

    def assemble(k, _):
        build(k)
        after(k, LATE)
        return 0

    lax.fori_loop(0, K, assemble, 0)

    def chunk(c, _):
        @pl.when(c < 4)
        def _():
            multiply(c)
            unsort(c)
            begin(c)

        @pl.when((c >= 1) & (c < 5))
        def _():
            middle(c - 1)

        @pl.when(c >= 2)
        def _():
            finish(c - 2)

        return 0

    lax.fori_loop(0, 6, chunk, 0)
    for c in range(4):
        close(c)

    def drain(c, _):
        for part in range(2):
            for sends in first_axis(part, c) + (second_axis(part, c),):
                for send in sends:
                    send.wait_send()
        return 0

    lax.fori_loop(0, 4, drain, 0)
    for i, ref in enumerate((X.at[pl.ds(0, 3), pl.ds(0, 7)], X.at[pl.ds(0, 3), pl.ds(0, 7)], X.at[:, pl.ds(0, 8)])):
        pltpu.make_async_copy(ref, ref, ring_send.at[i]).wait()


def call(m, s, cid, amplitudes, w, blockmap, irrep_virt, irrep_occ):
    hbm = pl.BlockSpec(memory_space=pl.ANY)
    vmem = pl.BlockSpec(memory_space=pltpu.VMEM)
    smem = pl.BlockSpec(memory_space=pltpu.SMEM)
    DMA = pltpu.SemaphoreType.DMA
    mp = m + m % 2
    rows = 64 * (m + s)
    out = pl.pallas_call(
        functools.partial(kernel, m, s),
        out_shape=jax.ShapeDtypeStruct((32, 8, 128), F32),
        in_specs=[hbm, hbm, vmem, smem, smem],
        out_specs=vmem,
        scratch_shapes=[
            pltpu.VMEM((K, 32, 512), F32),
            pltpu.VMEM((K, 16, 16 * m, 128), F32),
            pltpu.VMEM((K, 4096, 128), F32),
            pltpu.VMEM((K, NB, 64, 1024), BF16),
            pltpu.VMEM((K, NB, 64, 1024), BF16),
            pltpu.VMEM((K // 2, 2, 128 * mp, 1024), BF16),
            pltpu.VMEM((K // 2, 2, 128 * mp, 1024), BF16),
            pltpu.VMEM((12, 8, 8, 512), F32),
            pltpu.VMEM((rows, 64 * mp), F32),
            pltpu.VMEM((K // 2, rows, 128 * mp), BF16),
            pltpu.VMEM((K // 2, rows, 128 * mp), BF16),
            pltpu.VMEM((rows, 256), F32),
            pltpu.VMEM((4, 4, 32, 1024), F32),
            pltpu.VMEM((2, 4, 2, 2, 32, 128), F32),
            pltpu.VMEM((2, 4, 2, 2, 32, 128), F32),
            pltpu.VMEM((2, 4, 2, 2, 32, 128), F32),
            pltpu.VMEM((2, 4, 4, 32, 128), F32),
            pltpu.VMEM((2, 4, 3, 32, 128), F32),
            pltpu.SMEM((2 * SEL,), jnp.int32),
            DMA((K,)),
            DMA,
            DMA((K * 5,)),
            DMA((K * 5,)),
            DMA((K,)),
            DMA((3,)),
            DMA((72,)),
            DMA((72,)),
        ],
        cost_estimate=pl.CostEstimate(flops=10 ** 10, bytes_accessed=14 * 10 ** 6, transcendentals=0),
        compiler_params=pltpu.CompilerParams(
            collective_id=cid, has_side_effects=True, vmem_limit_bytes=60 * 1024 * 1024),
    )(amplitudes, w, blockmap, irrep_virt, irrep_occ)
    return out.reshape(32, 4, 2, 128).transpose(0, 2, 1, 3).reshape(32, 2, 512)


def dense_kernel(amp, w, bm, lv, lo_ref, out, X, Wf, Wh, Wl, bmx, Ch, Cl, acc, RA, RB, RD, S, QA, QB, QD,
           w_sem, x_sem, right_recv, left_recv, sib_recv, ring_send, rs_send, rs_recv):
    t = lax.axis_index("ta")
    wi = lax.axis_index("wa")
    z, h = t // 2, t % 2
    y, x = wi // 4, wi % 4

    def chip(delta):
        return lax.rem(z + delta + CHIPS, CHIPS)

    z_right = {"ta": chip(1) * 2 + h}
    z_left = {"ta": chip(-1) * 2 + h}
    sibling = {"ta": z * 2 + (1 - h)}

    def step(i, delta):
        return lax.rem(i + delta + 4, 4)

    x_next, x_prev = {"wa": y * 4 + step(x, 1)}, {"wa": y * 4 + step(x, -1)}
    y_next, y_prev = {"wa": step(y, 1) * 4 + x}, {"wa": step(y, -1) * 4 + x}

    def rows(zz, hh):
        return pl.ds(pl.multiple_of(zz * 64 + hh * 32, 32), 32)

    own = [
        pltpu.make_async_copy(amp.at[:, :, pl.ds(256 * g, 256)], X.at[:, g, rows(z, h), :], x_sem.at[g])
        for g in range(2)
    ]
    for c in own:
        c.start()

    def w_copy(k):
        return pltpu.make_async_copy(w.at[k], Wf.at[k], w_sem.at[k])

    for k in range(K):
        w_copy(k).start()

    barrier = pltpu.get_barrier_semaphore()
    neighbours = (z_right, z_left, sibling, x_next, x_prev, y_next, y_prev)
    for d in neighbours:
        pl.semaphore_signal(barrier, inc=1, device_id=d, device_id_type=MESH)

    lane = lax.broadcasted_iota(jnp.int32, (8, 512), 1) // 64
    row = lax.broadcasted_iota(jnp.int32, (8, 512), 0)
    spread = jnp.where(lane == row, 1.0, 0.0).astype(BF16)
    blocks = bm[...].astype(F32).reshape(96, 8).astype(BF16)
    bmx[...] = jnp.dot(blocks, spread, preferred_element_type=F32).reshape(12, 8, 512)
    acc[...] = jnp.zeros_like(acc)

    for c in own:
        c.wait()
    pl.semaphore_wait(barrier, len(neighbours))

    def unit_copy(u, zz, recv_sem, dest, direction):
        ref = X.at[u // 2, u % 2, rows(zz, h), :]
        return pltpu.make_async_remote_copy(
            src_ref=ref, dst_ref=ref, send_sem=ring_send.at[direction], recv_sem=recv_sem,
            device_id=dest, device_id_type=MESH)

    def to_right(u, zz, d):
        return unit_copy(u, zz, right_recv.at[u * 5 + d], z_right, 0)

    def to_left(u, zz, d):
        return unit_copy(u, zz, left_recv.at[u * 5 + d], z_left, 1)

    def to_sibling(u, zz):
        return unit_copy(u, zz, sib_recv.at[u // 2], sibling, 2)

    def w_prep(k):
        for r in range(8):
            bt, j = r // 2, r % 2
            for cb in range(8):
                slab = Wf[k, pl.ds(cb * 512 + r, 64, stride=8), :]
                m = bmx[k * 2 + j, pl.ds(cb, 1), pl.ds(bt * 128, 128)]
                hi, lo = split(slab * m)
                Wh[k, pl.ds(cb * 64, 64), pl.ds(r * 128, 128)] = hi
                Wl[k, pl.ds(cb * 64, 64), pl.ds(r * 128, 128)] = lo

    def compute(k, mh):
        lk = lo_ref[wi * K + k]
        blk = lax.broadcasted_iota(jnp.int32, (1, 256), 1) // 64
        for g in range(2):
            labels = jnp.zeros((1, 256), jnp.int32)
            for i in range(4):
                labels = jnp.where(blk == i, lv[(4 * g + i) * 64], labels)
            bt = X[k, mh, pl.ds(256 * g, 256), :].T
            for i in range(4):
                a = X[k, g, pl.ds(pl.multiple_of(256 * mh + 64 * i, 64), 64), :]
                lz = lv[(4 * mh + i) * 64]
                mask = ((labels + (lz + lk)) & 1) == 0
                c = jnp.where(mask, 2.0 * a - bt[64 * i:64 * i + 64, :], 0.0)
                hi, lo = split(c)
                Ch[pl.ds(64 * i, 64), pl.ds(256 * g, 256)] = hi
                Cl[pl.ds(64 * i, 64), pl.ds(256 * g, 256)] = lo
        for nb in range(4):
            n = pl.ds(256 * nb, 256)
            wh = Wh[k, :, n]
            p = jnp.dot(Ch[...], wh, preferred_element_type=F32)
            p = p + jnp.dot(Cl[...], wh, preferred_element_type=F32)
            p = p + jnp.dot(Ch[...], Wl[k, :, n], preferred_element_type=F32)
            acc[pl.ds(2 * mh, 2), :, :, n] += p.reshape(2, 4, 32, 256)

    def tick(s, _):
        @pl.when(s < UNITS)
        def _():
            to_right(s, z, 1).start()
            to_left(s, z, 1).start()
            to_sibling(s, z).start()

        for d in range(1, 5):
            u = s - LAG * d
            inside = (u >= 0) & (u < UNITS)
            even = u % 2 == 0

            @pl.when(inside if d < 4 else inside & even)
            def _():
                zz = chip(-d)
                to_right(u, zz, d).wait_recv()
                if d < 3:
                    to_right(u, zz, d + 1).start()
                elif d == 3:
                    @pl.when(even)
                    def _():
                        to_right(u, zz, d + 1).start()
                to_sibling(u, zz).start()

            @pl.when(inside if d < 4 else inside & jnp.logical_not(even))
            def _():
                zz = chip(d)
                to_left(u, zz, d).wait_recv()
                if d < 3:
                    to_left(u, zz, d + 1).start()
                elif d == 3:
                    @pl.when(jnp.logical_not(even))
                    def _():
                        to_left(u, zz, d + 1).start()
                to_sibling(u, zz).start()

        @pl.when((s >= 1) & (s < 1 + K))
        def _():
            k = s - 1
            w_copy(k).wait()
            w_prep(k)

        v = s - DELAY

        @pl.when((v >= 0) & (v < UNITS))
        def _():
            k, mh = v // 2, v % 2

            @pl.when(mh == 0)
            def _():
                ref = X.at[k, 0]
                pltpu.make_async_copy(ref, ref, sib_recv.at[k]).wait()

            compute(k, mh)

        return 0

    lax.fori_loop(0, UNITS + DELAY, tick, 0)

    def ring_sum(me, nxt, prv, view, bufs, base, result):
        a, b, d = bufs

        def copy(src, dst, i, dest):
            return pltpu.make_async_remote_copy(
                src_ref=src, dst_ref=dst, send_sem=rs_send.at[base + i], recv_sem=rs_recv.at[base + i],
                device_id=dest, device_id_type=MESH)

        first = [
            copy(view(step(me, 2), 0), a.at[0], 0, nxt),
            copy(view(step(me, 2), 1), a.at[1], 1, prv),
            copy(view(step(me, 1), 1), b.at[1], 2, nxt),
            copy(view(step(me, -1), 0), b.at[0], 3, prv),
        ]
        second = [
            copy(view(step(me, 1), 0), d.at[0], 4, nxt),
            copy(view(step(me, -1), 1), d.at[1], 5, prv),
        ]

        def start():
            for c in first:
                c.start()

        def middle():
            for i in range(2):
                first[i].wait_recv()
                ref = view(step(me, 1 if i == 0 else -1), i)
                ref[...] = ref[...] + a[i]
                second[i].start()

        def finish():
            first[2].wait_recv()
            first[3].wait_recv()
            for i in range(2):
                second[i].wait_recv()
                result(i, view(me, i)[...] + b[i] + d[i])

        def drain():
            for c in first + second:
                c.wait_send()

        return start, middle, finish, drain

    def cols(half, i):
        return pl.ds(512 * half + 256 * i, 256)

    def keep(half):
        def result(i, value):
            S[half, i] = value
        return result

    def emit(half):
        def result(i, value):
            for q in range(2):
                out[:, 4 * half + 2 * i + q, :] = value[:, 128 * q:128 * q + 128]
        return result

    def bufs(refs, half):
        return [r.at[half] for r in refs]

    one = [
        ring_sum(x, x_next, x_prev, lambda i, s: acc.at[:, i, :, cols(0, s)], bufs((RA, RB, RD), 0), 0, keep(0)),
        ring_sum(y, y_next, y_prev, lambda i, s: acc.at[i, :, :, cols(1, s)], bufs((RA, RB, RD), 1), 6, keep(1)),
    ]
    two = [
        ring_sum(y, y_next, y_prev, lambda i, s: S.at[0, s, i], bufs((QA, QB, QD), 0), 12, emit(0)),
        ring_sum(x, x_next, x_prev, lambda i, s: S.at[1, s, i], bufs((QA, QB, QD), 1), 18, emit(1)),
    ]
    for p in one:
        p[0]()
    for p in one:
        p[1]()
    for p, q in zip(one, two):
        p[2]()
        q[0]()
    for q in two:
        q[1]()
    for q in two:
        q[2]()
    for p in one + two:
        p[3]()
    for i, ref in enumerate((X.at[:, 0, pl.ds(0, 224), :], X.at[:, 0, pl.ds(0, 224), :], X.at[:, :, pl.ds(0, 256), :])):
        pltpu.make_async_copy(ref, ref, ring_send.at[i]).wait()


def dense_call(cid, amplitudes, w, blockmap, irrep_virt, irrep_occ):
    hbm = pl.BlockSpec(memory_space=pl.ANY)
    vmem = pl.BlockSpec(memory_space=pltpu.VMEM)
    smem = pl.BlockSpec(memory_space=pltpu.SMEM)
    DMA = pltpu.SemaphoreType.DMA
    out = pl.pallas_call(
        dense_kernel,
        out_shape=jax.ShapeDtypeStruct((32, 8, 128), F32),
        in_specs=[hbm, hbm, vmem, smem, smem],
        out_specs=vmem,
        scratch_shapes=[
            pltpu.VMEM((6, 2, 512, 256), F32),
            pltpu.VMEM((6, 4096, 128), F32),
            pltpu.VMEM((6, 512, 1024), BF16),
            pltpu.VMEM((6, 512, 1024), BF16),
            pltpu.VMEM((12, 8, 512), F32),
            pltpu.VMEM((256, 512), BF16),
            pltpu.VMEM((256, 512), BF16),
            pltpu.VMEM((4, 4, 32, 1024), F32),
            pltpu.VMEM((2, 2, 4, 32, 256), F32),
            pltpu.VMEM((2, 2, 4, 32, 256), F32),
            pltpu.VMEM((2, 2, 4, 32, 256), F32),
            pltpu.VMEM((2, 2, 4, 32, 256), F32),
            pltpu.VMEM((2, 2, 32, 256), F32),
            pltpu.VMEM((2, 2, 32, 256), F32),
            pltpu.VMEM((2, 2, 32, 256), F32),
            DMA((6,)),
            DMA((2,)),
            DMA((UNITS * 5,)),
            DMA((UNITS * 5,)),
            DMA((6,)),
            DMA((3,)),
            DMA((24,)),
            DMA((24,)),
        ],
        cost_estimate=pl.CostEstimate(flops=10 ** 10, bytes_accessed=14 * 10 ** 6, transcendentals=0),
        compiler_params=pltpu.CompilerParams(
            collective_id=cid, has_side_effects=True, vmem_limit_bytes=60 * 1024 * 1024),
    )(amplitudes, w, blockmap, irrep_virt, irrep_occ)
    return out.reshape(32, 4, 2, 128).transpose(0, 2, 1, 3).reshape(32, 2, 512)


SIZES = ((4, 4), (5, 3), (6, 2))


def local(amplitudes, integrals, blockmap, irrep_occ, irrep_virt):
    w = integrals.reshape(6, 512, 2, 4, 128).transpose(0, 1, 3, 2, 4).reshape(6, 4096, 128)
    ones = jnp.right_shift(jnp.sum(irrep_virt), 6)
    which = jnp.minimum(jnp.maximum(ones, NB - ones) - 4, len(SIZES))
    branches = [functools.partial(call, m, s, i) for i, (m, s) in enumerate(SIZES)]
    branches.append(functools.partial(dense_call, len(SIZES)))
    return lax.switch(which, branches, amplitudes, w, blockmap, irrep_virt, irrep_occ)


def solution(mesh):
    in_specs = (P("wa", "ta", None), P("wa", None, "ta", None), P("wa", "ta", None, None), P(), P())
    out_specs = P("wa", "ta", None)
    return jax.shard_map(local, mesh=mesh, in_specs=in_specs, out_specs=out_specs, check_vma=False)
```

```python
import functools

import jax
import jax.numpy as jnp
from jax import lax
from jax.experimental import pallas as pl
from jax.experimental.pallas import tpu as pltpu
from jax.sharding import PartitionSpec as P

MESH = pl.DeviceIdType.MESH
K = 6
CHIPS = 8
NB = 8
F32 = jnp.float32
BF16 = jnp.bfloat16
LAG = 2
UNITS = 2 * K
DELAY = 1 + 4 * LAG
FAR_RIGHT = (0, 2, 5)
EARLY = (((0, 1), (1, 1)), ((2, 1), (3, 1)), ((4, 1), (0, 2), (5, 1), (1, 2)), ((2, 2), (3, 2)),
         ((0, 3), (4, 2), (5, 2), (1, 3)), ((2, 3), (0, 4), (3, 3), (4, 3), (5, 3), (1, 4)))
LATE = (((2, 4),), ((3, 4),), ((5, 4), (4, 4)), (), (), ())
ROW = 16
SEL = 8 * ROW


def split(v):
    hi = v.astype(BF16)
    lo = (v - hi.astype(F32)).astype(BF16)
    return hi, lo


def kernel(m, s, amp, w, bm, lv, lo_ref, out, A, X, Wf, Vh, Vl, Wh, Wl, bmx, Z, Ch, Cl, accS, acc, RA, RB, RD, S, QD,
           tab, w_sem, x_sem, right_recv, left_recv, sib_recv, ring_send, rs_send, rs_recv):
    t = lax.axis_index("ta")
    wi = lax.axis_index("wa")
    z, h = t // 2, t % 2
    y, x = wi // 4, wi % 4
    mp = m + m % 2
    width = 64 * mp

    def chip(delta):
        return lax.rem(z + delta + CHIPS, CHIPS)

    z_right = {"ta": chip(1) * 2 + h}
    z_left = {"ta": chip(-1) * 2 + h}
    sibling = {"ta": z * 2 + (1 - h)}

    def step(i, delta):
        return lax.rem(i + delta + 4, 4)

    x_next, x_prev = {"wa": y * 4 + step(x, 1)}, {"wa": y * 4 + step(x, -1)}
    y_next, y_prev = {"wa": step(y, 1) * 4 + x}, {"wa": step(y, -1) * 4 + x}
    x_far, y_far = {"wa": y * 4 + step(x, 2)}, {"wa": step(y, 2) * 4 + x}

    own = pltpu.make_async_copy(amp, A, x_sem)
    own.start()

    def w_copy(k):
        return pltpu.make_async_copy(w.at[k], Wf.at[k, pl.ds(0, 4096)], w_sem.at[k])

    for k in range(K):
        w_copy(k).start()

    barrier = pltpu.get_barrier_semaphore()
    neighbours = (z_right, z_left, sibling, x_next, x_prev, x_far, y_next, y_prev, y_far)
    for d in neighbours:
        pl.semaphore_signal(barrier, inc=1, device_id=d, device_id_type=MESH)

    labels = [lv[64 * b] for b in range(NB)]
    ones = sum(labels)
    large = jnp.where(ones > NB // 2, 1, 0)
    member = [jnp.where(l == large, 0, 1) for l in labels]
    small_before = [sum(member[:b]) if b else jnp.int32(0) for b in range(NB)]
    rank = [jnp.where(member[b] == 1, small_before[b], b - small_before[b]) for b in range(NB)]
    small = sum(member)
    for g in range(2):
        for i in range(NB):
            for b in range(ROW):
                hit = (member[b] == g) & (rank[b] == i) if i <= b < NB else None
                tab[g * SEL + i * ROW + b] = jnp.int32(0) if hit is None else jnp.where(hit, 1, 0)

    def chosen(g, i, b, shape):
        return jnp.broadcast_to(tab[g * SEL + i * ROW + b], shape) == 1

    def chosen_either(g, lk, i, b, shape):
        one, two = tab[g * SEL + i * ROW + b], tab[(1 - g) * SEL + i * ROW + b]
        return jnp.broadcast_to(one + lk * (two - one), shape) == 1

    def size(g, lk):
        one, two = (NB - small, small) if g == 0 else (small, NB - small)
        return one + lk * (two - one)

    def span(g):
        return NB - (m, s)[g] + 1

    widest = NB - min(m, s) + 1

    def label_of(k):
        return lo_ref[wi * K + k]

    half = lax.broadcasted_iota(jnp.int32, (16, 128), 1) < 64
    own.wait()
    mine = jnp.where(lv[z * 64] == large, 0, 1)

    def pack(k):
        lk = label_of(k)
        group = mine + lk - 2 * mine * lk
        packed = []
        for b in range(NB):
            top, low = A[k, pl.ds(0, 16), pl.ds(b // 2 * 128, 128)], A[k, pl.ds(16, 16), pl.ds(b // 2 * 128, 128)]
            if b % 2:
                top = pltpu.roll(top, 64, 1)
            else:
                low = pltpu.roll(low, 64, 1)
            packed.append(jnp.where(half, top, low))
        for j in range(m):
            value = jnp.zeros((16, 128), F32)
            for b in range(j, min(j + widest, NB)):
                value = jnp.where(chosen_either(0, group, j, b, (16, 128)), packed[b], value)
            X[k, t, pl.ds(16 * j, 16), :] = value

    def unit_copy(u, zz, recv_sem, dest, direction):
        ref = X.at[u, zz * 2 + h]
        return pltpu.make_async_remote_copy(
            src_ref=ref, dst_ref=ref, send_sem=ring_send.at[direction], recv_sem=recv_sem,
            device_id=dest, device_id_type=MESH)

    def to_right(u, zz, d):
        return unit_copy(u, zz, right_recv.at[u * 5 + d], z_right, 0)

    def to_left(u, zz, d):
        return unit_copy(u, zz, left_recv.at[u * 5 + d], z_left, 1)

    def to_sibling(u, zz):
        return unit_copy(u, zz, sib_recv.at[u], sibling, 2)

    def send_own(u, _):
        pack(u)

        @pl.when(u == 0)
        def _():
            pl.semaphore_wait(barrier, len(neighbours))

        to_right(u, z, 1).start()
        to_left(u, z, 1).start()
        to_sibling(u, z).start()
        return 0

    def forward(u, d):
        for side, sign, reach in ((to_right, -1, 4 if u in FAR_RIGHT else 3), (to_left, 1, 3 if u in FAR_RIGHT else 4)):
            if d <= reach:
                side(u, chip(sign * d), d).wait_recv()
                if d < reach:
                    side(u, chip(sign * d), d + 1).start()
                to_sibling(u, chip(sign * d)).start()

    def after(i, moves):
        for j, some in enumerate(moves):
            if some:
                @pl.when(i == j)
                def _():
                    for u, d in some:
                        forward(u, d)

    def w_prep(k):
        w_copy(k).wait()

        def block(i, _):
            for r in range(8):
                bt, j = r // 2, r % 2
                slab = Wf[k, pl.ds(i * 512 + r, 64, stride=8), :]
                mask = bmx[k * 2 + j, i, :, pl.ds(bt * 128, 128)]
                hi, lo = split(slab * jnp.concatenate([mask] * 8, axis=0))
                Vh[k, i, :, pl.ds(r * 128, 128)] = hi
                Vl[k, i, :, pl.ds(r * 128, 128)] = lo
            return 0

        lax.fori_loop(0, NB, block, 0)
        lk = label_of(k)
        for g in range(2):
            def arrange(i, _):
                at = pl.ds(pl.multiple_of((k % 2) * width + i * 64, 64), 64)
                hit = [chosen_either(g, lk, i, i + o, (64, 256)) for o in range(widest)]
                for V, W in ((Vh, Wh), (Vl, Wl)):
                    for c in range(4):
                        value = jnp.zeros((64, 256), BF16)
                        for o in range(widest):
                            value = jnp.where(hit[o], V[k, jnp.minimum(i + o, NB - 1), :, pl.ds(256 * c, 256)], value)
                        W[k // 2, g, at, pl.ds(256 * c, 256)] = value
                return 0

            lax.fori_loop(0, mp, arrange, 0)

    groups = ((0, m, 0), (1, s, 64 * m))

    def build(k):
        ref = X.at[k, pl.ds(0, CHIPS)]
        pltpu.make_async_copy(ref, ref, sib_recv.at[k]).wait()

        for g, count, row0 in groups:
            def unpack(i, _):
                for core in range(2):
                    value = jnp.zeros((16 * m, 128), F32)
                    for o in range(span(g)):
                        b = jnp.minimum(i + o, NB - 1)
                        value = jnp.where(chosen(g, i, i + o, (16 * m, 128)), X[k, 2 * b + core], value)
                    at = row0 + 64 * i + 32 * core
                    for p in range(mp // 2):
                        one = value[32 * p:32 * p + 16]
                        two = value[32 * p + 16:32 * p + 32] if 2 * p + 1 < m else jnp.zeros((16, 128), F32)
                        cols = pl.ds(128 * p, 128)
                        Z[pl.ds(pl.multiple_of(at, 16), 16), cols] = jnp.where(half, one, pltpu.roll(two, 64, 1))
                        Z[pl.ds(pl.multiple_of(at + 16, 16), 16), cols] = jnp.where(half, pltpu.roll(one, 64, 1), two)
                return 0

            lax.fori_loop(0, count, unpack, 0)
        lk = label_of(k)
        into = pl.ds(pl.multiple_of(width * (k % 2), 128), width)
        for g, count, row0 in groups:
            wide = 64 * (count + count % 2)
            big = Z[pl.ds(0, 64 * m), pl.ds(0, wide)]
            few = jnp.concatenate([Z[pl.ds(64 * m, 64 * s), pl.ds(0, wide)]] + [jnp.zeros((64, wide), F32)] * (m - s), axis=0)
            pick = jnp.broadcast_to(lk, (64 * m, wide)) == g
            turned = jnp.where(pick, big, few)
            if mp > m:
                turned = jnp.concatenate([turned, jnp.zeros((64, wide), F32)], axis=0)
            turned = turned.T
            keep = lax.broadcasted_iota(jnp.int32, (64, width), 1) < size(g, lk) * 64
            for i in range(count):
                a = Z[pl.ds(row0 + 64 * i, 64), :]
                c = jnp.where(keep, 2.0 * a - turned[64 * i:64 * i + 64, :], 0.0)
                hi, lo = split(c)
                Ch[k // 2, pl.ds(row0 + 64 * i, 64), into] = hi
                Cl[k // 2, pl.ds(row0 + 64 * i, 64), into] = lo

    def multiply(c):
        n = pl.ds(pl.multiple_of(c * 256, 256), 256)

        def pair(q, _):
            for g, count, row0 in groups:
                rows = pl.ds(row0, 64 * count)
                wh = Wh[q, g, :, n]
                p = jnp.dot(Ch[q, rows, :], wh, preferred_element_type=F32)
                p = p + jnp.dot(Cl[q, rows, :], wh, preferred_element_type=F32)
                p = p + jnp.dot(Ch[q, rows, :], Wl[q, g, :, n], preferred_element_type=F32)
                accS[rows, :] = jnp.where(q == 0, p, accS[rows, :] + p)
            return 0

        lax.fori_loop(0, K // 2, pair, 0)

    def unsort(c):
        cols = pl.ds(pl.multiple_of(256 * c, 256), 256)

        for b in range(NB):
            value = None
            for g, count, row0 in groups:
                for i in range(max(0, b - span(g) + 1), min(b + 1, count)):
                    rows = accS[pl.ds(row0 + 64 * i, 64), :]
                    value = rows if value is None else jnp.where(chosen(g, i, b, (64, 256)), rows, value)
            acc[b // 2, pl.ds(2 * (b % 2), 2), :, cols] = value.reshape(2, 32, 256)

    lax.fori_loop(0, K, send_own, 0)
    lane = lax.broadcasted_iota(jnp.int32, (8, 512), 1) // 64
    row = lax.broadcasted_iota(jnp.int32, (8, 512), 0)
    spread = jnp.where(lane == row, 1.0, 0.0).astype(BF16)
    blocks = jnp.broadcast_to(bm[...].astype(F32).reshape(96, 1, 8), (96, 8, 8)).reshape(768, 8).astype(BF16)
    bmx[...] = jnp.dot(blocks, spread, preferred_element_type=F32).reshape(12, 8, 8, 512)

    accS[...] = jnp.zeros_like(accS)

    def prepare(k, _):
        w_prep(k)
        after(k, EARLY)
        return 0

    lax.fori_loop(0, K, prepare, 0)

    def copy(src, dst, i, dest):
        return pltpu.make_async_remote_copy(
            src_ref=src, dst_ref=dst, send_sem=rs_send.at[i], recv_sem=rs_recv.at[i],
            device_id=dest, device_id_type=MESH)

    along = ((x, x_next, x_prev, x_far), (y, y_next, y_prev, y_far))

    def view(part, c, i, side):
        cols = pl.ds(pl.multiple_of(256 * c + 128 * part, 128), 128)
        two = pl.ds(2 * side, 2)
        return acc.at[two, i, :, cols] if part == 0 else acc.at[i, two, :, cols]

    def first_axis(part, c):
        me, nxt, prv, _ = along[part]
        base = (4 * part + c) * 9
        a, b, d = (r.at[part, c] for r in (RA, RB, RD))
        far, up, down = step(me, 2), step(me, 1), step(me, -1)
        through = [copy(view(part, c, far, 0), a.at[0], base, nxt), copy(view(part, c, far, 1), a.at[1], base + 1, prv)]
        plain = [copy(view(part, c, down, 0), b.at[0], base + 2, prv), copy(view(part, c, up, 1), b.at[1], base + 3, nxt)]
        added = [copy(view(part, c, up, 0), d.at[0], base + 4, nxt), copy(view(part, c, down, 1), d.at[1], base + 5, prv)]
        return through, plain, added

    def second_axis(part, c):
        me, nxt, prv, far = along[1 - part]
        base = (4 * part + c) * 9 + 6
        return [copy(S.at[part, c, step(me, i + 1)], QD.at[part, c, i], base + i, dest)
                for i, dest in enumerate((nxt, far, prv))]

    def begin(c):
        stages = [first_axis(part, c) for part in range(2)]
        for order in range(2):
            for part in range(2):
                for send in stages[part][order]:
                    send.start()

    def middle(c):
        for part in range(2):
            me = along[part][0]
            through, _, added = first_axis(part, c)
            for i in range(2):
                through[i].wait_recv()
                view(part, c, step(me, 1 - 2 * i), i)[...] += RA[part, c, i]
                added[i].start()

    def finish(c):
        for part in range(2):
            me = along[part][0]
            _, plain, added = first_axis(part, c)
            for i in range(2):
                plain[i].wait_recv()
                added[i].wait_recv()
                S[part, c, pl.ds(2 * i, 2)] = view(part, c, me, i)[...] + RB[part, c, i] + RD[part, c, i]
            for send in second_axis(part, c):
                send.start()

    def close(c):
        for part in range(2):
            for send in second_axis(part, c):
                send.wait_recv()
            total = S[part, c, along[1 - part][0]] + QD[part, c, 0] + QD[part, c, 1] + QD[part, c, 2]
            out[:, 2 * c + part, :] = total

    def assemble(k, _):
        build(k)
        after(k, LATE)
        return 0

    lax.fori_loop(0, K, assemble, 0)

    def chunk(c, _):
        @pl.when(c < 4)
        def _():
            multiply(c)
            unsort(c)
            begin(c)

        @pl.when((c >= 1) & (c < 5))
        def _():
            middle(c - 1)

        @pl.when(c >= 2)
        def _():
            finish(c - 2)

        return 0

    lax.fori_loop(0, 6, chunk, 0)
    for c in range(4):
        close(c)

    def drain(c, _):
        for part in range(2):
            for sends in first_axis(part, c) + (second_axis(part, c),):
                for send in sends:
                    send.wait_send()
        return 0

    lax.fori_loop(0, 4, drain, 0)
    for i, ref in enumerate((X.at[pl.ds(0, 3), pl.ds(0, 7)], X.at[pl.ds(0, 3), pl.ds(0, 7)], X.at[:, pl.ds(0, 8)])):
        pltpu.make_async_copy(ref, ref, ring_send.at[i]).wait()


def call(m, s, cid, amplitudes, w, blockmap, irrep_virt, irrep_occ):
    hbm = pl.BlockSpec(memory_space=pl.ANY)
    vmem = pl.BlockSpec(memory_space=pltpu.VMEM)
    smem = pl.BlockSpec(memory_space=pltpu.SMEM)
    DMA = pltpu.SemaphoreType.DMA
    mp = m + m % 2
    rows = 64 * (m + s)
    out = pl.pallas_call(
        functools.partial(kernel, m, s),
        out_shape=jax.ShapeDtypeStruct((32, 8, 128), F32),
        in_specs=[hbm, hbm, vmem, smem, smem],
        out_specs=vmem,
        scratch_shapes=[
            pltpu.VMEM((K, 32, 512), F32),
            pltpu.VMEM((K, 16, 16 * m, 128), F32),
            pltpu.VMEM((K, 4104, 128), F32),
            pltpu.VMEM((K, NB, 64, 1024), BF16),
            pltpu.VMEM((K, NB, 64, 1024), BF16),
            pltpu.VMEM((K // 2, 2, 128 * mp, 1024), BF16),
            pltpu.VMEM((K // 2, 2, 128 * mp, 1024), BF16),
            pltpu.VMEM((12, 8, 8, 512), F32),
            pltpu.VMEM((rows, 64 * mp), F32),
            pltpu.VMEM((K // 2, rows, 128 * mp), BF16),
            pltpu.VMEM((K // 2, rows, 128 * mp), BF16),
            pltpu.VMEM((rows, 256), F32),
            pltpu.VMEM((4, 4, 32, 1024), F32),
            pltpu.VMEM((2, 4, 2, 2, 32, 128), F32),
            pltpu.VMEM((2, 4, 2, 2, 32, 128), F32),
            pltpu.VMEM((2, 4, 2, 2, 32, 128), F32),
            pltpu.VMEM((2, 4, 4, 32, 128), F32),
            pltpu.VMEM((2, 4, 3, 32, 128), F32),
            pltpu.SMEM((2 * SEL,), jnp.int32),
            DMA((K,)),
            DMA,
            DMA((K * 5,)),
            DMA((K * 5,)),
            DMA((K,)),
            DMA((3,)),
            DMA((72,)),
            DMA((72,)),
        ],
        cost_estimate=pl.CostEstimate(flops=10 ** 10, bytes_accessed=14 * 10 ** 6, transcendentals=0),
        compiler_params=pltpu.CompilerParams(
            collective_id=cid, has_side_effects=True, vmem_limit_bytes=60 * 1024 * 1024),
    )(amplitudes, w, blockmap, irrep_virt, irrep_occ)
    return out.reshape(32, 4, 2, 128).transpose(0, 2, 1, 3).reshape(32, 2, 512)


def dense_kernel(amp, w, bm, lv, lo_ref, out, X, Wf, Wh, Wl, bmx, Ch, Cl, acc, RA, RB, RD, S, QA, QB, QD,
           w_sem, x_sem, right_recv, left_recv, sib_recv, ring_send, rs_send, rs_recv):
    t = lax.axis_index("ta")
    wi = lax.axis_index("wa")
    z, h = t // 2, t % 2
    y, x = wi // 4, wi % 4

    def chip(delta):
        return lax.rem(z + delta + CHIPS, CHIPS)

    z_right = {"ta": chip(1) * 2 + h}
    z_left = {"ta": chip(-1) * 2 + h}
    sibling = {"ta": z * 2 + (1 - h)}

    def step(i, delta):
        return lax.rem(i + delta + 4, 4)

    x_next, x_prev = {"wa": y * 4 + step(x, 1)}, {"wa": y * 4 + step(x, -1)}
    y_next, y_prev = {"wa": step(y, 1) * 4 + x}, {"wa": step(y, -1) * 4 + x}

    def rows(zz, hh):
        return pl.ds(pl.multiple_of(zz * 64 + hh * 32, 32), 32)

    own = [
        pltpu.make_async_copy(amp.at[:, :, pl.ds(256 * g, 256)], X.at[:, g, rows(z, h), :], x_sem.at[g])
        for g in range(2)
    ]
    for c in own:
        c.start()

    def w_copy(k):
        return pltpu.make_async_copy(w.at[k], Wf.at[k, pl.ds(0, 4096)], w_sem.at[k])

    for k in range(K):
        w_copy(k).start()

    barrier = pltpu.get_barrier_semaphore()
    neighbours = (z_right, z_left, sibling, x_next, x_prev, y_next, y_prev)
    for d in neighbours:
        pl.semaphore_signal(barrier, inc=1, device_id=d, device_id_type=MESH)

    lane = lax.broadcasted_iota(jnp.int32, (8, 512), 1) // 64
    row = lax.broadcasted_iota(jnp.int32, (8, 512), 0)
    spread = jnp.where(lane == row, 1.0, 0.0).astype(BF16)
    blocks = bm[...].astype(F32).reshape(96, 8).astype(BF16)
    bmx[...] = jnp.dot(blocks, spread, preferred_element_type=F32).reshape(12, 8, 512)
    acc[...] = jnp.zeros_like(acc)

    for c in own:
        c.wait()
    pl.semaphore_wait(barrier, len(neighbours))

    def unit_copy(u, zz, recv_sem, dest, direction):
        ref = X.at[u // 2, u % 2, rows(zz, h), :]
        return pltpu.make_async_remote_copy(
            src_ref=ref, dst_ref=ref, send_sem=ring_send.at[direction], recv_sem=recv_sem,
            device_id=dest, device_id_type=MESH)

    def to_right(u, zz, d):
        return unit_copy(u, zz, right_recv.at[u * 5 + d], z_right, 0)

    def to_left(u, zz, d):
        return unit_copy(u, zz, left_recv.at[u * 5 + d], z_left, 1)

    def to_sibling(u, zz):
        return unit_copy(u, zz, sib_recv.at[u // 2], sibling, 2)

    def w_prep(k):
        for r in range(8):
            bt, j = r // 2, r % 2
            for cb in range(8):
                slab = Wf[k, pl.ds(cb * 512 + r, 64, stride=8), :]
                m = bmx[k * 2 + j, pl.ds(cb, 1), pl.ds(bt * 128, 128)]
                hi, lo = split(slab * m)
                Wh[k, pl.ds(cb * 64, 64), pl.ds(r * 128, 128)] = hi
                Wl[k, pl.ds(cb * 64, 64), pl.ds(r * 128, 128)] = lo

    def compute(k, mh):
        lk = lo_ref[wi * K + k]
        blk = lax.broadcasted_iota(jnp.int32, (1, 256), 1) // 64
        for g in range(2):
            labels = jnp.zeros((1, 256), jnp.int32)
            for i in range(4):
                labels = jnp.where(blk == i, lv[(4 * g + i) * 64], labels)
            bt = X[k, mh, pl.ds(256 * g, 256), :].T
            for i in range(4):
                a = X[k, g, pl.ds(pl.multiple_of(256 * mh + 64 * i, 64), 64), :]
                lz = lv[(4 * mh + i) * 64]
                mask = ((labels + (lz + lk)) & 1) == 0
                c = jnp.where(mask, 2.0 * a - bt[64 * i:64 * i + 64, :], 0.0)
                hi, lo = split(c)
                Ch[pl.ds(64 * i, 64), pl.ds(256 * g, 256)] = hi
                Cl[pl.ds(64 * i, 64), pl.ds(256 * g, 256)] = lo
        for nb in range(4):
            n = pl.ds(256 * nb, 256)
            wh = Wh[k, :, n]
            p = jnp.dot(Ch[...], wh, preferred_element_type=F32)
            p = p + jnp.dot(Cl[...], wh, preferred_element_type=F32)
            p = p + jnp.dot(Ch[...], Wl[k, :, n], preferred_element_type=F32)
            acc[pl.ds(2 * mh, 2), :, :, n] += p.reshape(2, 4, 32, 256)

    def tick(s, _):
        @pl.when(s < UNITS)
        def _():
            to_right(s, z, 1).start()
            to_left(s, z, 1).start()
            to_sibling(s, z).start()

        for d in range(1, 5):
            u = s - LAG * d
            inside = (u >= 0) & (u < UNITS)
            even = u % 2 == 0

            @pl.when(inside if d < 4 else inside & even)
            def _():
                zz = chip(-d)
                to_right(u, zz, d).wait_recv()
                if d < 3:
                    to_right(u, zz, d + 1).start()
                elif d == 3:
                    @pl.when(even)
                    def _():
                        to_right(u, zz, d + 1).start()
                to_sibling(u, zz).start()

            @pl.when(inside if d < 4 else inside & jnp.logical_not(even))
            def _():
                zz = chip(d)
                to_left(u, zz, d).wait_recv()
                if d < 3:
                    to_left(u, zz, d + 1).start()
                elif d == 3:
                    @pl.when(jnp.logical_not(even))
                    def _():
                        to_left(u, zz, d + 1).start()
                to_sibling(u, zz).start()

        @pl.when((s >= 1) & (s < 1 + K))
        def _():
            k = s - 1
            w_copy(k).wait()
            w_prep(k)

        v = s - DELAY

        @pl.when((v >= 0) & (v < UNITS))
        def _():
            k, mh = v // 2, v % 2

            @pl.when(mh == 0)
            def _():
                ref = X.at[k, 0]
                pltpu.make_async_copy(ref, ref, sib_recv.at[k]).wait()

            compute(k, mh)

        return 0

    lax.fori_loop(0, UNITS + DELAY, tick, 0)

    def ring_sum(me, nxt, prv, view, bufs, base, result):
        a, b, d = bufs

        def copy(src, dst, i, dest):
            return pltpu.make_async_remote_copy(
                src_ref=src, dst_ref=dst, send_sem=rs_send.at[base + i], recv_sem=rs_recv.at[base + i],
                device_id=dest, device_id_type=MESH)

        first = [
            copy(view(step(me, 2), 0), a.at[0], 0, nxt),
            copy(view(step(me, 2), 1), a.at[1], 1, prv),
            copy(view(step(me, 1), 1), b.at[1], 2, nxt),
            copy(view(step(me, -1), 0), b.at[0], 3, prv),
        ]
        second = [
            copy(view(step(me, 1), 0), d.at[0], 4, nxt),
            copy(view(step(me, -1), 1), d.at[1], 5, prv),
        ]

        def start():
            for c in first:
                c.start()

        def middle():
            for i in range(2):
                first[i].wait_recv()
                ref = view(step(me, 1 if i == 0 else -1), i)
                ref[...] = ref[...] + a[i]
                second[i].start()

        def finish():
            first[2].wait_recv()
            first[3].wait_recv()
            for i in range(2):
                second[i].wait_recv()
                result(i, view(me, i)[...] + b[i] + d[i])

        def drain():
            for c in first + second:
                c.wait_send()

        return start, middle, finish, drain

    def cols(half, i):
        return pl.ds(512 * half + 256 * i, 256)

    def keep(half):
        def result(i, value):
            S[half, i] = value
        return result

    def emit(half):
        def result(i, value):
            for q in range(2):
                out[:, 4 * half + 2 * i + q, :] = value[:, 128 * q:128 * q + 128]
        return result

    def bufs(refs, half):
        return [r.at[half] for r in refs]

    one = [
        ring_sum(x, x_next, x_prev, lambda i, s: acc.at[:, i, :, cols(0, s)], bufs((RA, RB, RD), 0), 0, keep(0)),
        ring_sum(y, y_next, y_prev, lambda i, s: acc.at[i, :, :, cols(1, s)], bufs((RA, RB, RD), 1), 6, keep(1)),
    ]
    two = [
        ring_sum(y, y_next, y_prev, lambda i, s: S.at[0, s, i], bufs((QA, QB, QD), 0), 12, emit(0)),
        ring_sum(x, x_next, x_prev, lambda i, s: S.at[1, s, i], bufs((QA, QB, QD), 1), 18, emit(1)),
    ]
    for p in one:
        p[0]()
    for p in one:
        p[1]()
    for p, q in zip(one, two):
        p[2]()
        q[0]()
    for q in two:
        q[1]()
    for q in two:
        q[2]()
    for p in one + two:
        p[3]()
    for i, ref in enumerate((X.at[:, 0, pl.ds(0, 224), :], X.at[:, 0, pl.ds(0, 224), :], X.at[:, :, pl.ds(0, 256), :])):
        pltpu.make_async_copy(ref, ref, ring_send.at[i]).wait()


def dense_call(cid, amplitudes, w, blockmap, irrep_virt, irrep_occ):
    hbm = pl.BlockSpec(memory_space=pl.ANY)
    vmem = pl.BlockSpec(memory_space=pltpu.VMEM)
    smem = pl.BlockSpec(memory_space=pltpu.SMEM)
    DMA = pltpu.SemaphoreType.DMA
    out = pl.pallas_call(
        dense_kernel,
        out_shape=jax.ShapeDtypeStruct((32, 8, 128), F32),
        in_specs=[hbm, hbm, vmem, smem, smem],
        out_specs=vmem,
        scratch_shapes=[
            pltpu.VMEM((6, 2, 512, 256), F32),
            pltpu.VMEM((6, 4104, 128), F32),
            pltpu.VMEM((6, 512, 1024), BF16),
            pltpu.VMEM((6, 512, 1024), BF16),
            pltpu.VMEM((12, 8, 512), F32),
            pltpu.VMEM((256, 512), BF16),
            pltpu.VMEM((256, 512), BF16),
            pltpu.VMEM((4, 4, 32, 1024), F32),
            pltpu.VMEM((2, 2, 4, 32, 256), F32),
            pltpu.VMEM((2, 2, 4, 32, 256), F32),
            pltpu.VMEM((2, 2, 4, 32, 256), F32),
            pltpu.VMEM((2, 2, 4, 32, 256), F32),
            pltpu.VMEM((2, 2, 32, 256), F32),
            pltpu.VMEM((2, 2, 32, 256), F32),
            pltpu.VMEM((2, 2, 32, 256), F32),
            DMA((6,)),
            DMA((2,)),
            DMA((UNITS * 5,)),
            DMA((UNITS * 5,)),
            DMA((6,)),
            DMA((3,)),
            DMA((24,)),
            DMA((24,)),
        ],
        cost_estimate=pl.CostEstimate(flops=10 ** 10, bytes_accessed=14 * 10 ** 6, transcendentals=0),
        compiler_params=pltpu.CompilerParams(
            collective_id=cid, has_side_effects=True, vmem_limit_bytes=60 * 1024 * 1024),
    )(amplitudes, w, blockmap, irrep_virt, irrep_occ)
    return out.reshape(32, 4, 2, 128).transpose(0, 2, 1, 3).reshape(32, 2, 512)


SIZES = ((4, 4), (5, 3), (6, 2))


def local(amplitudes, integrals, blockmap, irrep_occ, irrep_virt):
    w = integrals.reshape(6, 512, 2, 4, 128).transpose(0, 1, 3, 2, 4).reshape(6, 4096, 128)
    ones = jnp.right_shift(jnp.sum(irrep_virt), 6)
    which = jnp.minimum(jnp.maximum(ones, NB - ones) - 4, len(SIZES))
    branches = [functools.partial(call, m, s, i) for i, (m, s) in enumerate(SIZES)]
    branches.append(functools.partial(dense_call, len(SIZES)))
    return lax.switch(which, branches, amplitudes, w, blockmap, irrep_virt, irrep_occ)


def solution(mesh):
    in_specs = (P("wa", "ta", None), P("wa", None, "ta", None), P("wa", "ta", None, None), P(), P())
    out_specs = P("wa", "ta", None)
    return jax.shard_map(local, mesh=mesh, in_specs=in_specs, out_specs=out_specs, check_vma=False)
```
